32 devices in a mesh: dp: 4 (over z), ctx: 4 (over x, core), tp: 2 (over y).
Axes of the slice: x: 2, y: 2, z: 4, core: 2. Of those that a mesh axis runs over, the one named last changes fastest.
Arguments:
- latents_in: bfloat16 [12, 1024, 768], P('dp', 'ctx'), may hold values from -6 to 6
- condition: float32 [12, 768], P('dp'), may hold values from -6 to 6
- out_grad: bfloat16 [12, 1024, 768], P('dp', 'ctx'), may hold values from -6 to 6
- mod_weight: bfloat16 [2, 768, 4608], P(None, 'dp', 'tp'), may hold values from -0.21875 to 0.21875
- mod_bias: bfloat16 [2, 6, 768], P(None, 'tp', 'dp'), may hold values from -3 to 3
- qkv_weight: bfloat16 [2, 3, 768, 768], P(None, None, 'dp', 'tp'), may hold values from -0.21875 to 0.21875
- qkv_bias: bfloat16 [2, 2, 12, 64], P(None, None, 'tp', 'dp'), may hold values from -3 to 3
- proj_weight: bfloat16 [2, 768, 768], P(None, 'dp', 'tp'), may hold values from -2.5 to 2.5
- proj_bias: bfloat16 [2, 768], P(None, 'dp'), may hold values from -3 to 3
- fc1_weight: bfloat16 [2, 768, 3072], P(None, 'dp', 'tp'), may hold values from -0.21875 to 0.21875
- fc1_bias: bfloat16 [2, 24, 128], P(None, 'tp', 'dp'), may hold values from -3 to 3
- fc2_weight: bfloat16 [2, 768, 3072], P(None, 'dp', 'tp'), may hold values from -0.109375 to 0.109375
- fc2_bias: bfloat16 [2, 768], P(None, 'dp'), may hold values from -3 to 3
Outputs:
- block_out: bfloat16 [12, 1024, 768], P('dp', 'ctx')
- latents_grad: float32 [12, 1024, 768], P('dp', 'ctx')
- condition_grad: float32 [12, 768], P('dp')
- mod_weight_grad: float32 [2, 768, 4608], P(None, 'dp', 'tp')
- mod_bias_grad: float32 [2, 6, 768], P(None, 'tp', 'dp')
- qkv_weight_grad: float32 [2, 3, 768, 768], P(None, None, 'dp', 'tp')
- qkv_bias_grad: float32 [2, 2, 12, 64], P(None, None, 'tp', 'dp')
- proj_weight_grad: float32 [2, 768, 768], P(None, 'dp', 'tp')
- proj_bias_grad: float32 [2, 768], P(None, 'dp')
- fc1_weight_grad: float32 [2, 768, 3072], P(None, 'dp', 'tp')
- fc1_bias_grad: float32 [2, 24, 128], P(None, 'tp', 'dp')
- fc2_weight_grad: float32 [2, 768, 3072], P(None, 'dp', 'tp')
- fc2_bias_grad: float32 [2, 768], P(None, 'dp')
The draws below stay inside these ranges and needn't reach their ends.
All inputs are finite; a program needn't handle non-finite values.
Results may differ from the reference program's by a relative error of at most 0.02.
The reference program's roundings to bfloat16 on the way count: a program that leaves them out, or rounds other values in their place, can miss the bound.
Values may be sent and summed in bfloat16 or wider, within the bound.
No kernel may reach another device: no remote copies, remote signals or barrier semaphores. Data moves between devices by JAX's collectives and lax.ppermute only.
A program may use at most 256 MiB of HBM per device.

```python
import jax
import jax.numpy as jnp
from jax import lax

D = 768
HEADS = 12
HD = 64
FF = 3072
LAYERS = 2
SEQ = 1024
LATENTS = 12


def level_of(rng, shape, split, low, top_value):
    factor_of = 1.0
    for axis_at, parts in split:
        heights = jax.random.uniform(jax.random.fold_in(jax.random.fold_in(rng, 6), axis_at), (parts,), jnp.float32, low / len(split), top_value / len(split))
        factor_of = factor_of * jnp.repeat(jnp.exp(heights), shape[axis_at] // parts).reshape((-1,) + (1,) * (len(shape) - 1 - axis_at))
    return factor_of


def scatter_about(key, shape, width, limit, shards=(), kind=jnp.bfloat16):
    entries = jax.random.normal(key, shape, jnp.float32) * width
    if len(shards) > 0:
        entries = level_of(key, shape, shards, -0.22, 0.18) * entries
    return jnp.clip(entries, min=-limit, max=limit).astype(kind)


def setup_inputs(seed: int = 0) -> dict:
    splits = jax.random.split(jax.random.key(seed), 14)
    latents_in = scatter_about(splits[0], (LATENTS, SEQ, D), 1.0, 6.0, ((0, 4), (1, 4)))
    condition = scatter_about(splits[1], (LATENTS, D), 1.0, 6.0, ((0, 4),), jnp.float32)
    out_grad = scatter_about(splits[2], (LATENTS, SEQ, D), 1.0, 6.0, ((0, 4), (1, 4)))
    mod_weight = scatter_about(splits[3], (LAYERS, D, 6 * D), D ** -0.5, 0.21875, ((1, 4), (2, 2)))
    mod_bias = scatter_about(splits[4], (LAYERS, 6, D), 0.5, 3.0, ((1, 2), (2, 4)))
    qkv_weight = scatter_about(splits[5], (LAYERS, 3, D, D), D ** -0.5, 0.21875, ((2, 4), (3, 2)))
    qkv_bias = scatter_about(splits[6], (LAYERS, 2, HEADS, HD), 0.5, 3.0, ((2, 2), (3, 4)))
    proj_weight = scatter_about(splits[7], (LAYERS, D, D), (max(D // 128, 1)) ** -0.5, 2.5, ((1, 4), (2, 2)))
    proj_bias = scatter_about(splits[8], (LAYERS, D), 0.5, 3.0, ((1, 4),))
    fc1_weight = scatter_about(splits[9], (LAYERS, D, FF), D ** -0.5, 0.21875, ((1, 4), (2, 2)))
    fc1_bias = scatter_about(splits[10], (LAYERS, FF // 128, 128), 0.5, 3.0, ((1, 2), (2, 4)))
    fc2_weight = scatter_about(splits[11], (LAYERS, D, FF), FF ** -0.5, 0.109375, ((1, 4), (2, 2)))
    fc2_bias = scatter_about(splits[12], (LAYERS, D), 0.5, 3.0, ((1, 4),))
    return dict(latents_in=latents_in, condition=condition, out_grad=out_grad, mod_weight=mod_weight, mod_bias=mod_bias, qkv_weight=qkv_weight, qkv_bias=qkv_bias, proj_weight=proj_weight, proj_bias=proj_bias, fc1_weight=fc1_weight, fc1_bias=fc1_bias, fc2_weight=fc2_weight, fc2_bias=fc2_bias)


@jax.custom_vjp
def low(v):
    return lax.optimization_barrier(v.astype(jnp.bfloat16)).astype(jnp.float32)

@jax.custom_vjp
def low_back(v):
    return v

def low_keep(v):
    return (low(v), None)

def low_pass(kept, grad):
    return (grad,)

def back_keep(v):
    return (v, None)

def back_low(kept, grad):
    return (low(grad),)
low.defvjp(low_keep, low_pass)
low_back.defvjp(back_keep, back_low)
PRECISE = lax.Precision.HIGHEST
EPSILON = 1e-06

def normalize(field):
    centre = field - lax.optimization_barrier(jnp.mean(field, axis=-1, keepdims=True))
    return centre * lax.rsqrt(lax.optimization_barrier(jnp.mean(centre * centre, axis=-1, keepdims=True)) + EPSILON)

def attend(triple):
    queries, keyset, values = triple
    raw_scores = jnp.einsum('hqd,hkd->hqk', queries, keyset, precision=PRECISE)
    scores = low_back(raw_scores) * HD ** (-0.5)
    probs = low(jax.nn.softmax(scores, axis=-1))
    return jnp.einsum('hqk,hkd->hqd', probs, values, precision=PRECISE)

def heads_first(field):
    return field.reshape(field.shape[0], SEQ, HEADS, HD).transpose(0, 2, 1, 3)

def block_forward(resid, silu_cond, mod_w, mod_b, qkv_w, qkv_b, proj_w, proj_b, up_w, up_b, down_w, down_b):
    count = resid.shape[0]
    modulation = (jnp.dot(silu_cond, mod_w, precision=PRECISE) + mod_b.reshape(-1)).reshape(count, 6, D)
    shift_one = modulation[:, 0:1, :]
    scale_one = modulation[:, 1:2, :]
    gate_one = modulation[:, 2:3, :]
    shift_two = modulation[:, 3:4, :]
    scale_two = modulation[:, 4:5, :]
    gate_two = modulation[:, 5:6, :]
    entry_one = low(normalize(resid) * (1.0 + scale_one) + shift_one)
    projected = jnp.einsum('bsd,tde->tbse', entry_one, qkv_w, precision=PRECISE)
    bias_flat = qkv_b.reshape(2, D)
    queries = low(low_back(projected[0] + bias_flat[0]))
    keyset = low(low_back(projected[1]))
    values = low(low_back(projected[2] + bias_flat[1]))
    context = lax.map(jax.checkpoint(attend), (heads_first(queries), heads_first(keyset), heads_first(values)))
    context = low(low_back(context.transpose(0, 2, 1, 3).reshape(count, SEQ, D)))
    attended = low_back(jnp.einsum('bsi,oi->bso', context, proj_w, precision=PRECISE) + proj_b)
    middle = resid + gate_one * attended
    entry_two = low(normalize(middle) * (1.0 + scale_two) + shift_two)
    hidden_pre = low_back(jnp.einsum('bsd,df->bsf', entry_two, up_w, precision=PRECISE) + up_b.reshape(-1))
    hidden = low(jax.nn.gelu(hidden_pre, approximate=True))
    mlp_out = low_back(jnp.einsum('bsf,of->bso', hidden, down_w, precision=PRECISE) + down_b)
    return middle + gate_two * mlp_out

def reference(latents_in, condition, out_grad, mod_weight, mod_bias, qkv_weight, qkv_bias, proj_weight, proj_bias, fc1_weight, fc1_bias, fc2_weight, fc2_bias):
    params = [member.astype(jnp.float32) for member in (mod_weight, mod_bias, qkv_weight, qkv_bias, proj_weight, proj_bias, fc1_weight, fc1_bias, fc2_weight, fc2_bias)]

    def forward(resid, cond, *weights):
        silu_cond = jax.nn.silu(cond)
        for layer_no in range(LAYERS):
            resid = block_forward(resid, silu_cond, *[member[layer_no] for member in weights])
        return resid
    result, pull = jax.vjp(forward, latents_in.astype(jnp.float32), condition.astype(jnp.float32), *params)
    grads = pull(out_grad.astype(jnp.float32))
    return (result.astype(jnp.bfloat16), grads[0], grads[1], grads[2], grads[3], grads[4], grads[5], grads[6], grads[7], grads[8], grads[9], grads[10], grads[11])
```

```python
import jax
import jax.numpy as jnp
from jax import lax
from jax.experimental import pallas as pl
from jax.experimental.pallas import tpu as pltpu
from jax.sharding import PartitionSpec as P

PRECISE = lax.Precision.HIGHEST
EPSILON = 1e-06
LOW = jnp.bfloat16
FULL = jnp.float32
CHIPS = ((0, 0), (0, 1), (1, 0), (1, 1))
PLANE = ("ctx", "tp")
VMEM_LIMIT = 56 * 1024 * 1024


def swap(value, x=0, core=0, y=0):
    mask = 4 * x + 2 * core + y
    return lax.ppermute(value, PLANE, [(at, at ^ mask) for at in range(8)])


def swap_dp(value, mask, count):
    return lax.ppermute(value, "dp", [(at, at ^ mask) for at in range(count)])


def pick(index, options):
    if len(options) == 1:
        return options[0]
    half = len(options) // 2
    low, high = pick(index % half, options[:half]), pick(index % half, options[half:])
    return jnp.where(index // half == 0, low, high)


def unrelate(pieces, index):
    return [pick(index, [pieces[place ^ at] for at in range(len(pieces))]) for place in range(len(pieces))]


class Place:
    def __init__(self, mesh):
        self.n_dp = mesh.shape["dp"]
        self.z = lax.axis_index("dp")
        self.ctx = lax.axis_index("ctx")
        self.x = self.ctx // 2
        self.core = self.ctx % 2
        self.y = lax.axis_index("tp")
        self.direct = self.n_dp <= 4 and self.n_dp & (self.n_dp - 1) == 0

    def gather_dp(self, value):
        if not self.direct:
            return lax.all_gather(value, "dp")
        pieces = [value] + [swap_dp(value, mask, self.n_dp) for mask in range(1, self.n_dp)]
        return jnp.stack(unrelate(pieces, self.z))

    def scatter_dp(self, value, dtype):
        if not self.direct:
            return lax.psum_scatter(value.astype(dtype), "dp", scatter_dimension=0).astype(FULL)
        total = lax.dynamic_index_in_dim(value, self.z, 0, keepdims=False)
        for mask in range(1, self.n_dp):
            part = lax.dynamic_index_in_dim(value, self.z ^ mask, 0, keepdims=False)
            total = total + swap_dp(part.astype(dtype), mask, self.n_dp).astype(FULL)
        return total

    def sum_plane(self, value):
        value = value + swap(value, core=1)
        value = value + swap(value, x=1)
        return value + swap(value, y=1)


def normalize(field):
    centre = field - jnp.mean(field, axis=-1, keepdims=True)
    scaling = lax.rsqrt(jnp.mean(centre * centre, axis=-1, keepdims=True) + EPSILON)
    return (centre * scaling, scaling)


def norm_back(upstream, normed, scaling):
    first = jnp.mean(upstream, axis=-1, keepdims=True)
    second = jnp.mean(upstream * normed, axis=-1, keepdims=True)
    return scaling * (upstream - first - normed * second)


def activation(field):
    return jax.nn.gelu(field, approximate=True)


def dot(left, right):
    return jnp.dot(left, right, preferred_element_type=FULL)


def dot_nt(left, right):
    return lax.dot_general(left, right, (((1,), (1,)), ((), ())), preferred_element_type=FULL)


def dot_tn(left, right):
    return lax.dot_general(left, right, (((0,), (0,)), ((), ())), preferred_element_type=FULL)


def attend_kernel(size, factor, own_ref, other_ref, out_ref, log_ref):
    chips, tokens, triple = own_ref.shape
    width = triple // 3
    own = own_ref[...].reshape(chips * tokens, triple)
    other = other_ref[...].reshape(chips * tokens, 2 * width)
    outs = []
    for head in range(width // size):
        lo, hi = head * size, (head + 1) * size
        queries = own[:, lo:hi] * jnp.asarray(factor, LOW)
        score_a = dot_nt(queries, own[:, width + lo : width + hi])
        score_b = dot_nt(queries, other[:, lo:hi])
        highest = jnp.maximum(
            jnp.max(score_a, axis=-1, keepdims=True), jnp.max(score_b, axis=-1, keepdims=True)
        )
        exp_a = jnp.exp(score_a - highest)
        exp_b = jnp.exp(score_b - highest)
        total = jnp.sum(exp_a, axis=-1, keepdims=True) + jnp.sum(exp_b, axis=-1, keepdims=True)
        inverse = 1.0 / total
        out = dot((exp_a * inverse).astype(LOW), own[:, 2 * width + lo : 2 * width + hi])
        out = out + dot((exp_b * inverse).astype(LOW), other[:, width + lo : width + hi])
        outs.append(out)
        log_ref[:, head : head + 1] = highest + jnp.log(total)
    out_ref[...] = jnp.concatenate(outs, axis=1).astype(LOW).reshape(chips, tokens, width)


def attend(own, other, size):
    chips, latents, tokens, triple = own.shape
    width = triple // 3
    heads = width // size
    rows = chips * tokens

    def block(columns):
        return pl.BlockSpec((chips, None, tokens, columns), lambda at: (0, at, 0, 0))

    return pl.pallas_call(
        lambda *refs: attend_kernel(size, size**-0.5, *refs),
        grid=(latents,),
        in_specs=[block(triple), block(2 * width)],
        out_specs=[block(width), pl.BlockSpec((None, rows, heads), lambda at: (at, 0, 0))],
        out_shape=[
            jax.ShapeDtypeStruct((chips, latents, tokens, width), LOW),
            jax.ShapeDtypeStruct((latents, rows, heads), FULL),
        ],
        compiler_params=pltpu.CompilerParams(vmem_limit_bytes=VMEM_LIMIT),
        cost_estimate=pl.CostEstimate(
            flops=8 * latents * rows * rows * width,
            bytes_accessed=6 * 2 * latents * rows * width,
            transcendentals=2 * latents * heads * rows * rows,
        ),
        name="attention_forward",
    )(own, other)


def attend_back_kernel(
    size, factor, own_ref, other_ref, grad_ref, log_ref, query_ref, kv_own_ref, kv_other_ref
):
    chips, tokens, triple = own_ref.shape
    width = triple // 3
    rows = chips * tokens
    own = own_ref[...].reshape(rows, triple)
    other = other_ref[...].reshape(rows, 2 * width)
    grad = grad_ref[...].reshape(rows, width)
    query_grads, key_own, value_own, key_other, value_other = [], [], [], [], []
    for head in range(width // size):
        lo, hi = head * size, (head + 1) * size
        queries = own[:, lo:hi] * jnp.asarray(factor, LOW)
        upstream = grad[:, lo:hi]
        logsum = log_ref[:, head : head + 1]
        keys_a = own[:, width + lo : width + hi]
        keys_b = other[:, lo:hi]
        prob_a = jnp.exp(dot_nt(queries, keys_a) - logsum)
        prob_b = jnp.exp(dot_nt(queries, keys_b) - logsum)
        grad_a = dot_nt(upstream, own[:, 2 * width + lo : 2 * width + hi])
        grad_b = dot_nt(upstream, other[:, width + lo : width + hi])
        terms = jnp.sum(prob_a * grad_a, axis=-1, keepdims=True)
        terms = terms + jnp.sum(prob_b * grad_b, axis=-1, keepdims=True)
        score_a = (prob_a * (grad_a - terms)).astype(LOW)
        score_b = (prob_b * (grad_b - terms)).astype(LOW)
        query_grads.append((dot(score_a, keys_a) + dot(score_b, keys_b)) * factor)
        key_own.append(dot_tn(score_a, queries))
        key_other.append(dot_tn(score_b, queries))
        value_own.append(dot_tn(prob_a.astype(LOW), upstream))
        value_other.append(dot_tn(prob_b.astype(LOW), upstream))
    query_ref[...] = (
        jnp.concatenate(query_grads, axis=1).astype(LOW).reshape(chips, tokens, width)
    )
    kv_own_ref[...] = jnp.concatenate(key_own + value_own, axis=1).reshape(
        chips, tokens, 2 * width
    )
    kv_other_ref[...] = jnp.concatenate(key_other + value_other, axis=1).reshape(
        chips, tokens, 2 * width
    )


def attend_back(own, other, grad, logsum, size):
    chips, latents, tokens, triple = own.shape
    width = triple // 3
    heads = width // size
    rows = chips * tokens

    def block(columns):
        return pl.BlockSpec((chips, None, tokens, columns), lambda at: (0, at, 0, 0))

    def shape(columns, dtype):
        return jax.ShapeDtypeStruct((chips, latents, tokens, columns), dtype)

    return pl.pallas_call(
        lambda *refs: attend_back_kernel(size, size**-0.5, *refs),
        grid=(latents,),
        in_specs=[
            block(triple),
            block(2 * width),
            block(width),
            pl.BlockSpec((None, rows, heads), lambda at: (at, 0, 0)),
        ],
        out_specs=[block(width), block(2 * width), block(2 * width)],
        out_shape=[shape(width, LOW), shape(2 * width, FULL), shape(2 * width, FULL)],
        compiler_params=pltpu.CompilerParams(vmem_limit_bytes=VMEM_LIMIT),
        cost_estimate=pl.CostEstimate(
            flops=20 * latents * rows * rows * width,
            bytes_accessed=26 * latents * rows * width,
            transcendentals=2 * latents * heads * rows * rows,
        ),
        name="attention_backward",
    )(own, other, grad, logsum)


def spread_plane(unit, x_first):
    if x_first:
        over_x = swap(unit, x=1)
        pair = jnp.concatenate([unit, over_x], axis=1)
        far = swap(pair, y=1)
        width = unit.shape[1]
        quad = jnp.concatenate([unit, far[:, :width], over_x, far[:, width:]], axis=1)
    else:
        pair = jnp.concatenate([unit, swap(unit, y=1)], axis=1)
        quad = jnp.concatenate([pair, swap(pair, x=1)], axis=1)
    return (quad, swap(quad, core=1))


def fetch_weight(place, shard, x_first):
    whole = place.gather_dp(shard)
    return spread_plane(whole.reshape(-1, shard.shape[1]), x_first)


def collect_grad(place, own_terms, other_terms, x_first):
    width = own_terms.shape[1] // 4
    quad = own_terms + swap(other_terms.astype(LOW), core=1).astype(FULL)
    units = [quad[:, at * width : (at + 1) * width] for at in range(4)]
    if x_first:
        sent = jnp.concatenate([units[1], units[3]], axis=1).astype(LOW)
        pair = jnp.concatenate([units[0], units[2]], axis=1) + swap(sent, y=1).astype(FULL)
        unit = pair[:, :width] + swap(pair[:, width:].astype(LOW), x=1).astype(FULL)
    else:
        pair = quad[:, : 2 * width] + swap(quad[:, 2 * width :].astype(LOW), x=1).astype(FULL)
        unit = pair[:, :width] + swap(pair[:, width:].astype(LOW), y=1).astype(FULL)
    return place.scatter_dp(unit.reshape(place.n_dp, -1, width), LOW)


def spread_ctx(place, unit):
    over_x = swap(unit, x=1)
    far = swap(jnp.stack([unit, over_x]), core=1)
    return unrelate([unit, far[0], over_x, far[1]], place.ctx)


def to_chips(place, blocks):
    arrived = []
    for at, (x, y) in enumerate(CHIPS):
        block = jnp.where(place.x ^ x == 0, blocks[y][0], blocks[y][1])
        arrived.append(block if at == 0 else swap(block, x=x, y=y))
    return jnp.stack(arrived)


def from_chips(place, stacked):
    arrived = [
        stacked[at] if at == 0 else swap(stacked[at], x=x, y=y) for at, (x, y) in enumerate(CHIPS)
    ]
    by_group = []
    for y in range(2):
        near, far = arrived[y], arrived[2 + y]
        by_group.append(
            (jnp.where(place.x == 0, near, far), jnp.where(place.x == 0, far, near))
        )
    return by_group


def block_forward(place, resid, modulation, weights, biases, size):
    (attn_quads, up_quads, down_quads) = weights
    (query_bias, value_bias, proj_bias, up_bias, down_bias) = biases
    latents, tokens, width = resid.shape
    shift_one, scale_one, gate_one, shift_two, scale_two, gate_two = [
        modulation[:, at : at + 1, :] for at in range(6)
    ]
    (near, far) = attn_quads
    four = unrelate([near[:, :width], far[:, :width], near[:, width:], far[:, width:]], place.ctx)
    qkv_weight = jnp.concatenate(four[:3], axis=1)
    proj_weight = four[3]
    normed_one, scaling_one = normalize(resid)
    entry_one = (normed_one * (1.0 + scale_one) + shift_one).astype(LOW).reshape(-1, width)
    projected = dot(entry_one, qkv_weight)
    queries = (projected[:, :width] + query_bias).astype(LOW)
    keys = projected[:, width : 2 * width].astype(LOW)
    values = (projected[:, 2 * width :] + value_bias).astype(LOW)
    part = width // 4
    blocks = [
        [
            jnp.concatenate(
                [
                    member[:, (2 * rel + group) * part : (2 * rel + group + 1) * part]
                    for member in (queries, keys, values)
                ],
                axis=1,
            )
            for group in range(2)
        ]
        for rel in range(2)
    ]
    own = to_chips(place, blocks)
    other = swap(own[:, :, part:], core=1)
    own = own.reshape(4, latents, tokens, 3 * part)
    other = other.reshape(4, latents, tokens, 2 * part)
    attn_out, logsum = attend(own, other, size)
    pieces = from_chips(place, attn_out.reshape(4, latents * tokens, part))
    context = jnp.concatenate([*pieces[0], *pieces[1]], axis=1)
    attended = (dot_nt(context, proj_weight) + proj_bias).reshape(resid.shape)
    middle = resid + gate_one * attended
    normed_two, scaling_two = normalize(middle)
    entry_two = (normed_two * (1.0 + scale_two) + shift_two).astype(LOW).reshape(-1, width)
    hidden_pre = [dot(entry_two, up_quads[at]) + up_bias[at] for at in range(2)]
    hidden = [activation(member).astype(LOW) for member in hidden_pre]
    mlp_out = dot_nt(hidden[0], down_quads[0]) + dot_nt(hidden[1], down_quads[1])
    mlp_out = (mlp_out + down_bias).reshape(resid.shape)
    result = middle + gate_two * mlp_out
    saved = (
        normed_one,
        scaling_one,
        entry_one,
        own,
        other,
        logsum,
        context,
        attended,
        normed_two,
        scaling_two,
        entry_two,
        hidden_pre,
        hidden,
        mlp_out,
        qkv_weight,
        proj_weight,
    )
    return (result, saved)


def block_backward(place, upstream, modulation, weights, saved, size):
    (attn_quads, up_quads, down_quads) = weights
    (
        normed_one,
        scaling_one,
        entry_one,
        own,
        other,
        logsum,
        context,
        attended,
        normed_two,
        scaling_two,
        entry_two,
        hidden_pre,
        hidden,
        mlp_out,
        qkv_weight,
        proj_weight,
    ) = saved
    latents, tokens, width = upstream.shape
    part = width // 4
    shift_one, scale_one, gate_one, shift_two, scale_two, gate_two = [
        modulation[:, at : at + 1, :] for at in range(6)
    ]
    gate_two_grad = jnp.sum(upstream * mlp_out, axis=1)
    mlp_grad = (gate_two * upstream).astype(LOW).reshape(-1, width)
    down_bias_grad = jnp.sum(mlp_grad, axis=0, dtype=FULL)
    down_grad = [dot_tn(mlp_grad, member) for member in hidden]
    down_shard = collect_grad(place, down_grad[0], down_grad[1], True)
    pre_grad = []
    for at in range(2):
        unused_value, gelu_pull = jax.vjp(activation, hidden_pre[at])
        pre_grad.append(gelu_pull(dot(mlp_grad, down_quads[at]))[0].astype(LOW))
    up_bias_grad = [jnp.sum(member, axis=0, dtype=FULL) for member in pre_grad]
    up_grad = [dot_tn(entry_two, member) for member in pre_grad]
    up_shard = collect_grad(place, up_grad[0], up_grad[1], False)
    entry_two_grad = dot_nt(pre_grad[0], up_quads[0]) + dot_nt(pre_grad[1], up_quads[1])
    entry_two_grad = entry_two_grad.reshape(upstream.shape)
    scale_two_grad = jnp.sum(entry_two_grad * normed_two, axis=1)
    shift_two_grad = jnp.sum(entry_two_grad, axis=1)
    middle_grad = upstream + norm_back(entry_two_grad * (1.0 + scale_two), normed_two, scaling_two)
    gate_one_grad = jnp.sum(middle_grad * attended, axis=1)
    attended_grad = (gate_one * middle_grad).astype(LOW).reshape(-1, width)
    proj_bias_grad = jnp.sum(attended_grad, axis=0, dtype=FULL)
    context_grad = dot(attended_grad, proj_weight).astype(LOW)
    blocks = [
        [context_grad[:, (2 * rel + at) * part : (2 * rel + at + 1) * part] for at in range(2)]
        for rel in range(2)
    ]
    out_grad = to_chips(place, blocks).reshape(4, latents, tokens, part)
    query_part, kv_own, kv_other = attend_back(own, other, out_grad, logsum, size)
    kv_part = (kv_own + swap(kv_other, core=1)).astype(LOW)
    pieces = from_chips(
        place,
        jnp.concatenate([query_part, kv_part], axis=-1).reshape(4, latents * tokens, 3 * part),
    )
    ordered = [*pieces[0], *pieces[1]]
    triple = [
        jnp.concatenate([member[:, at * part : (at + 1) * part] for member in ordered], axis=1)
        for at in range(3)
    ]
    query_bias_grad = jnp.sum(triple[0], axis=0, dtype=FULL)
    value_bias_grad = jnp.sum(triple[2], axis=0, dtype=FULL)
    entry_one_grad = dot_nt(jnp.concatenate(triple, axis=1), qkv_weight).reshape(upstream.shape)
    scale_one_grad = jnp.sum(entry_one_grad * normed_one, axis=1)
    shift_one_grad = jnp.sum(entry_one_grad, axis=1)
    resid_grad = middle_grad + norm_back(
        entry_one_grad * (1.0 + scale_one), normed_one, scaling_one
    )
    rights = jnp.stack([*triple, context])
    terms = []
    for at in range(4):
        matrix = place.ctx ^ at
        left = jnp.where(matrix == 3, attended_grad, entry_one)
        terms.append(dot_tn(left, lax.dynamic_index_in_dim(rights, matrix, 0, keepdims=False)))
    attn_shard = collect_grad(
        place,
        jnp.concatenate([terms[0], terms[2]], axis=1),
        jnp.concatenate([terms[1], terms[3]], axis=1),
        False,
    )
    mod_grad = jnp.stack(
        [
            shift_one_grad,
            scale_one_grad,
            gate_one_grad,
            shift_two_grad,
            scale_two_grad,
            gate_two_grad,
        ],
        axis=1,
    )
    def halves(value):
        return jnp.concatenate(
            [
                jnp.where(place.y == 0, value[: width // 2], value[width // 2 :]),
                jnp.where(place.y == 0, value[width // 2 :], value[: width // 2]),
            ]
        )

    quarters = [member.reshape(2, 2, -1) for member in up_bias_grad]
    by_ctx = unrelate([quarters[0][0], quarters[1][0], quarters[0][1], quarters[1][1]], place.ctx)
    by_unit = jnp.stack(by_ctx, axis=1)
    up_bias_all = jnp.concatenate(
        [
            jnp.where(place.y == 0, by_unit[0], by_unit[1]).reshape(-1),
            jnp.where(place.y == 0, by_unit[1], by_unit[0]).reshape(-1),
        ]
    )
    bias_grad = jnp.concatenate(
        [halves(query_bias_grad), halves(value_bias_grad), proj_bias_grad, up_bias_all, down_bias_grad]
    )
    return (resid_grad, (attn_shard, up_shard, down_shard), mod_grad, bias_grad)


def local(
    mesh,
    latents_in,
    condition,
    out_grad,
    mod_weight,
    mod_bias,
    qkv_weight,
    qkv_bias,
    proj_weight,
    proj_bias,
    fc1_weight,
    fc1_bias,
    fc2_weight,
    fc2_bias,
):
    place = Place(mesh)
    n_dp = place.n_dp
    layers = mod_weight.shape[0]
    latents, ctx_tokens, width = latents_in.shape
    tokens = ctx_tokens // 2
    rows = width // n_dp
    heads = qkv_bias.shape[2]
    size = qkv_bias.shape[3] * n_dp
    quarter = fc1_weight.shape[2] // 4

    all_weights = []
    for layer in range(layers):
        attn = pick(place.ctx, [*[qkv_weight[layer, at] for at in range(3)], proj_weight[layer]])
        start = place.ctx * quarter
        up = lax.dynamic_slice_in_dim(fc1_weight[layer], start, quarter, 1)
        down = lax.dynamic_slice_in_dim(fc2_weight[layer], start, quarter, 1)
        all_weights.append(
            (
                fetch_weight(place, attn, False),
                fetch_weight(place, up, False),
                fetch_weight(place, down, True),
            )
        )

    members = (mod_bias, qkv_bias, proj_bias, fc1_bias, fc2_bias)
    flat = jnp.concatenate(
        [condition.reshape(-1), *[member.astype(FULL).reshape(-1) for member in members]]
    )
    everyone = place.gather_dp(flat)
    cond_all = everyone[:, : condition.size].reshape(n_dp * latents, width)
    bias_near = everyone[:, condition.size :]
    bias_both = jnp.stack([bias_near, swap(bias_near, y=1)])
    taken = []
    start = 0
    for member in members:
        taken.append(
            bias_both[:, :, start : start + member.size].reshape((2, n_dp) + member.shape)
        )
        start += member.size
    spans = mod_bias.shape[1]
    mod_bias_half = jnp.moveaxis(taken[0][0], 0, 2).reshape(layers, spans * width)
    qkv_bias_all = jnp.transpose(taken[1], (2, 3, 0, 4, 1, 5)).reshape(layers, 2, 2 * heads * size)
    proj_bias_all = jnp.moveaxis(taken[2][0], 0, 1).reshape(layers, width)
    fc1_all = jnp.transpose(taken[3], (2, 0, 3, 1, 4)).reshape(layers, 2, 4, quarter)
    fc2_bias_all = jnp.moveaxis(taken[4][0], 0, 1).reshape(layers, width)
    fc1_rel = jnp.stack(
        [
            lax.dynamic_index_in_dim(fc1_all, place.ctx ^ at, 2, keepdims=False)
            for at in range(4)
        ]
    )
    fc1_rel = fc1_rel.reshape(2, 2, layers, 2, quarter)

    silu_all = jax.nn.silu(cond_all)
    silu_rows = lax.dynamic_slice_in_dim(silu_all, place.z * rows, rows, 1)
    halfmod = jnp.einsum(
        "bd,lde->lbe", silu_rows, mod_weight.astype(FULL), precision=PRECISE
    ).reshape(layers, n_dp, latents, -1)
    halfmod = place.scatter_dp(jnp.moveaxis(halfmod, 1, 0), FULL) + mod_bias_half[:, None, :]
    farmod = swap(halfmod, y=1)
    modulation = jnp.concatenate(
        [jnp.where(place.y == 0, halfmod, farmod), jnp.where(place.y == 0, farmod, halfmod)],
        axis=-1,
    ).reshape(layers, latents, 2 * spans, width)

    token_start = place.y * tokens
    resid = lax.dynamic_slice_in_dim(latents_in, token_start, tokens, 1).astype(FULL)
    upstream = lax.dynamic_slice_in_dim(out_grad, token_start, tokens, 1).astype(FULL)
    saved_list = []
    for layer in range(layers):
        up_bias = [
            jnp.moveaxis(fc1_rel[:, core, layer], 0, 0).reshape(-1) for core in range(2)
        ]
        biases = (
            qkv_bias_all[layer, 0],
            qkv_bias_all[layer, 1],
            proj_bias_all[layer],
            up_bias,
            fc2_bias_all[layer],
        )
        resid, saved = block_forward(
            place, resid, modulation[layer], all_weights[layer], biases, size
        )
        saved_list.append(saved)

    def both_halves(value):
        other = swap(value, y=1)
        return jnp.concatenate(
            [jnp.where(place.y == 0, value, other), jnp.where(place.y == 0, other, value)], axis=1
        )

    block_out = both_halves(resid.astype(LOW))
    shards = [None] * layers
    mod_grads = [None] * layers
    bias_grads = [None] * layers
    for layer in reversed(range(layers)):
        upstream, shards[layer], mod_grads[layer], bias_grads[layer] = block_backward(
            place, upstream, modulation[layer], all_weights[layer], saved_list[layer], size
        )
    latents_grad = both_halves(upstream)

    mod_stack = jnp.stack(mod_grads)
    bias_stack = jnp.stack(bias_grads)
    vector = jnp.concatenate([mod_stack.reshape(-1), bias_stack.reshape(-1)])
    vectors = place.gather_dp(place.sum_plane(vector))
    mod_all = vectors[:, : mod_stack.size].reshape((n_dp,) + mod_stack.shape)
    mod_all = jnp.moveaxis(mod_all, 0, 1).reshape(layers, n_dp * latents, 2, -1)
    own_mod = lax.dynamic_index_in_dim(mod_all, place.y, 2, keepdims=False)
    mod_wgrad = jnp.einsum("bd,lbe->lde", silu_rows, own_mod, precision=PRECISE)
    mod_bsum = jnp.sum(own_mod, axis=1).reshape(layers, spans, n_dp, rows)
    mod_bgrad = lax.dynamic_index_in_dim(mod_bsum, place.z, 2, keepdims=False)
    cond_part = jnp.einsum("lbe,lde->bd", own_mod, mod_weight.astype(FULL), precision=PRECISE)
    cond_part = cond_part + swap(cond_part, y=1)
    cond_blocks = place.gather_dp(cond_part).reshape(n_dp, n_dp, latents, rows)
    cond_sum = lax.dynamic_index_in_dim(cond_blocks, place.z, 1, keepdims=False)
    cond_sum = jnp.moveaxis(cond_sum, 0, 1).reshape(latents, width)
    unused_value, silu_pull = jax.vjp(jax.nn.silu, condition)
    condition_grad = silu_pull(cond_sum)[0]

    bias_sum = jnp.sum(vectors[:, mod_stack.size :], axis=0).reshape(layers, -1)
    qkv_b = bias_sum[:, : 2 * width].reshape(layers, 2, 2, heads, n_dp, -1)
    qkv_b = lax.dynamic_index_in_dim(qkv_b, place.y, 2, keepdims=False)
    qkv_bgrad = lax.dynamic_index_in_dim(qkv_b, place.z, 3, keepdims=False)
    proj_bgrad = lax.dynamic_slice_in_dim(
        bias_sum[:, 2 * width : 3 * width], place.z * rows, rows, 1
    )
    fc1_b = bias_sum[:, 3 * width : -width].reshape((layers, 2, fc1_bias.shape[1], n_dp, -1))
    fc1_b = lax.dynamic_index_in_dim(fc1_b, place.y, 1, keepdims=False)
    fc1_bgrad = lax.dynamic_index_in_dim(fc1_b, place.z, 2, keepdims=False)
    fc2_bgrad = lax.dynamic_slice_in_dim(bias_sum[:, -width:], place.z * rows, rows, 1)

    qkv_wgrad, proj_wgrad, fc1_wgrad, fc2_wgrad = [], [], [], []
    for layer in range(layers):
        attn_units, up_units, down_units = [spread_ctx(place, member) for member in shards[layer]]
        qkv_wgrad.append(jnp.stack(attn_units[:3]))
        proj_wgrad.append(attn_units[3])
        fc1_wgrad.append(jnp.concatenate(up_units, axis=1))
        fc2_wgrad.append(jnp.concatenate(down_units, axis=1))
    return (
        block_out,
        latents_grad,
        condition_grad,
        mod_wgrad,
        mod_bgrad,
        jnp.stack(qkv_wgrad),
        qkv_bgrad,
        jnp.stack(proj_wgrad),
        proj_bgrad,
        jnp.stack(fc1_wgrad),
        fc1_bgrad,
        jnp.stack(fc2_wgrad),
        fc2_bgrad,
    )


def solution(mesh):
    placed = (
        P("dp", "ctx", None),
        P("dp", None),
        P("dp", "ctx", None),
        P(None, "dp", "tp"),
        P(None, "tp", "dp"),
        P(None, None, "dp", "tp"),
        P(None, None, "tp", "dp"),
        P(None, "dp", "tp"),
        P(None, "dp"),
        P(None, "dp", "tp"),
        P(None, "tp", "dp"),
        P(None, "dp", "tp"),
        P(None, "dp"),
    )
    outs = (
        P("dp", "ctx", None),
        P("dp", "ctx", None),
        P("dp", None),
        P(None, "dp", "tp"),
        P(None, "tp", "dp"),
        P(None, None, "dp", "tp"),
        P(None, None, "tp", "dp"),
        P(None, "dp", "tp"),
        P(None, "dp"),
        P(None, "dp", "tp"),
        P(None, "tp", "dp"),
        P(None, "dp", "tp"),
        P(None, "dp"),
    )
    return jax.shard_map(
        lambda *arrays: local(mesh, *arrays),
        mesh=mesh,
        in_specs=placed,
        out_specs=outs,
        check_vma=False,
    )
```

```python
import jax
import jax.numpy as jnp
from jax import lax
from jax.experimental import pallas as pl
from jax.experimental.pallas import tpu as pltpu
from jax.sharding import PartitionSpec as P

PRECISE = lax.Precision.HIGHEST
EPSILON = 1e-06
LOW = jnp.bfloat16
FULL = jnp.float32
CHIPS = ((0, 0), (0, 1), (1, 0), (1, 1))
PLANE = ("ctx", "tp")
VMEM_LIMIT = 56 * 1024 * 1024


def swap(value, x=0, core=0, y=0):
    mask = 4 * x + 2 * core + y
    return lax.ppermute(value, PLANE, [(at, at ^ mask) for at in range(8)])


def swap_dp(value, mask, count):
    return lax.ppermute(value, "dp", [(at, at ^ mask) for at in range(count)])


def pick(index, options):
    if len(options) == 1:
        return options[0]
    half = len(options) // 2
    low, high = pick(index % half, options[:half]), pick(index % half, options[half:])
    return jnp.where(index // half == 0, low, high)


def tie(value, after):
    if after is None:
        return value
    return lax.optimization_barrier((value, after))[0]


def unrelate(pieces, index):
    return [pick(index, [pieces[place ^ at] for at in range(len(pieces))]) for place in range(len(pieces))]


class Place:
    def __init__(self, mesh):
        self.n_dp = mesh.shape["dp"]
        self.z = lax.axis_index("dp")
        self.ctx = lax.axis_index("ctx")
        self.x = self.ctx // 2
        self.core = self.ctx % 2
        self.y = lax.axis_index("tp")
        self.direct = self.n_dp <= 4 and self.n_dp & (self.n_dp - 1) == 0

    def gather_dp(self, value):
        if not self.direct:
            return lax.all_gather(value, "dp")
        pieces = [value] + [swap_dp(value, mask, self.n_dp) for mask in range(1, self.n_dp)]
        return jnp.stack(unrelate(pieces, self.z))

    def scatter_dp(self, parts, dtype):
        if not self.direct:
            whole = jnp.stack([parts(at) for at in range(self.n_dp)]).astype(dtype)
            return lax.psum_scatter(whole, "dp", scatter_dimension=0).astype(FULL)
        total = parts(self.z)
        for mask in range(1, self.n_dp):
            part = parts(self.z ^ mask).astype(dtype)
            total = total + swap_dp(part, mask, self.n_dp).astype(FULL)
        return total

    def by_y(self, near, far):
        return (jnp.where(self.y == 0, near, far), jnp.where(self.y == 0, far, near))

    def unit_matrix(self):
        at = lax.broadcasted_iota(jnp.int32, (8, 8), 0)
        rel = lax.broadcasted_iota(jnp.int32, (8, 8), 1)
        flip_core = (at % 2) ^ self.core
        flip_x = (at // 2 % 2) ^ self.x
        flip_y = (at // 4) ^ self.y
        return (rel == 4 * flip_core + 2 * flip_x + flip_y).astype(FULL)


def normalize(field):
    centre = field - jnp.mean(field, axis=-1, keepdims=True)
    scaling = lax.rsqrt(jnp.mean(centre * centre, axis=-1, keepdims=True) + EPSILON)
    return (centre * scaling, scaling)


def norm_back(upstream, normed, scaling):
    first = jnp.mean(upstream, axis=-1, keepdims=True)
    second = jnp.mean(upstream * normed, axis=-1, keepdims=True)
    return scaling * (upstream - first - normed * second)


def activation(field):
    return jax.nn.gelu(field, approximate=True)


def dot(left, right):
    return jnp.dot(left, right, preferred_element_type=FULL)


def dot_nt(left, right):
    return lax.dot_general(left, right, (((1,), (1,)), ((), ())), preferred_element_type=FULL)


def dot_tn(left, right):
    return lax.dot_general(left, right, (((0,), (0,)), ((), ())), preferred_element_type=FULL)


def attend_kernel(size, factor, *refs):
    own_refs, other_refs, out_refs, log_ref = refs[:4], refs[4:8], refs[8:12], refs[12]
    tokens, triple = own_refs[0].shape
    width = triple // 3
    own = jnp.concatenate([ref[...] for ref in own_refs], axis=0)
    other = jnp.concatenate([ref[:, : 2 * width] for ref in other_refs], axis=0)
    outs = []
    for head in range(width // size):
        lo, hi = head * size, (head + 1) * size
        queries = own[:, 2 * width + lo : 2 * width + hi] * jnp.asarray(factor, LOW)
        score_a = dot_nt(queries, own[:, lo:hi])
        score_b = dot_nt(queries, other[:, lo:hi])
        highest = jnp.maximum(
            jnp.max(score_a, axis=-1, keepdims=True), jnp.max(score_b, axis=-1, keepdims=True)
        )
        exp_a = jnp.exp(score_a - highest)
        exp_b = jnp.exp(score_b - highest)
        total = jnp.sum(exp_a, axis=-1, keepdims=True) + jnp.sum(exp_b, axis=-1, keepdims=True)
        inverse = 1.0 / total
        out = dot((exp_a * inverse).astype(LOW), own[:, width + lo : width + hi])
        out = out + dot((exp_b * inverse).astype(LOW), other[:, width + lo : width + hi])
        outs.append(out)
        log_ref[:, head : head + 1] = highest + jnp.log(total)
    out = jnp.concatenate(outs, axis=1).astype(LOW)
    for at in range(4):
        out_refs[at][...] = out[at * tokens : (at + 1) * tokens]


def attend(own, other, size):
    latents, tokens, triple = own[0].shape
    width = triple // 3
    heads = width // size
    rows = 4 * tokens

    def block(columns):
        return pl.BlockSpec((None, tokens, columns), lambda at: (at, 0, 0))

    results = pl.pallas_call(
        lambda *refs: attend_kernel(size, size**-0.5, *refs),
        grid=(latents,),
        in_specs=[block(triple)] * 8,
        out_specs=[block(width)] * 4 + [pl.BlockSpec((None, rows, heads), lambda at: (at, 0, 0))],
        out_shape=[jax.ShapeDtypeStruct((latents, tokens, width), LOW)] * 4
        + [jax.ShapeDtypeStruct((latents, rows, heads), FULL)],
        compiler_params=pltpu.CompilerParams(vmem_limit_bytes=VMEM_LIMIT),
        cost_estimate=pl.CostEstimate(
            flops=8 * latents * rows * rows * width,
            bytes_accessed=14 * latents * rows * width,
            transcendentals=2 * latents * heads * rows * rows,
        ),
        name="attention_forward",
    )(*own, *other)
    return (results[:4], results[4])


def attend_back_kernel(size, factor, *refs):
    own_refs, other_refs, grad_refs, log_ref = refs[:4], refs[4:8], refs[8:12], refs[12]
    query_ref, kv_own_ref, kv_other_ref = refs[13:]
    tokens, triple = own_refs[0].shape
    width = triple // 3
    rows = 4 * tokens
    own = jnp.concatenate([ref[...] for ref in own_refs], axis=0)
    other = jnp.concatenate([ref[:, : 2 * width] for ref in other_refs], axis=0)
    grad = jnp.concatenate([ref[...] for ref in grad_refs], axis=0)
    query_grads, key_own, value_own, key_other, value_other = [], [], [], [], []
    for head in range(width // size):
        lo, hi = head * size, (head + 1) * size
        queries = own[:, 2 * width + lo : 2 * width + hi] * jnp.asarray(factor, LOW)
        upstream = grad[:, lo:hi]
        logsum = log_ref[:, head : head + 1]
        keys_a = own[:, lo:hi]
        keys_b = other[:, lo:hi]
        prob_a = jnp.exp(dot_nt(queries, keys_a) - logsum)
        prob_b = jnp.exp(dot_nt(queries, keys_b) - logsum)
        grad_a = dot_nt(upstream, own[:, width + lo : width + hi])
        grad_b = dot_nt(upstream, other[:, width + lo : width + hi])
        terms = jnp.sum(prob_a * grad_a, axis=-1, keepdims=True)
        terms = terms + jnp.sum(prob_b * grad_b, axis=-1, keepdims=True)
        score_a = (prob_a * (grad_a - terms)).astype(LOW)
        score_b = (prob_b * (grad_b - terms)).astype(LOW)
        query_grads.append((dot(score_a, keys_a) + dot(score_b, keys_b)) * factor)
        key_own.append(dot_tn(score_a, queries))
        key_other.append(dot_tn(score_b, queries))
        value_own.append(dot_tn(prob_a.astype(LOW), upstream))
        value_other.append(dot_tn(prob_b.astype(LOW), upstream))
    query_ref[...] = jnp.concatenate(query_grads, axis=1).astype(LOW).reshape(4, tokens, width)
    kv_own_ref[...] = jnp.concatenate(key_own + value_own, axis=1).reshape(4, tokens, 2 * width)
    kv_other_ref[...] = jnp.concatenate(key_other + value_other, axis=1).reshape(
        4, tokens, 2 * width
    )


def attend_back(own, other, grad, logsum, size):
    latents, tokens, triple = own[0].shape
    width = triple // 3
    heads = width // size
    rows = 4 * tokens

    def block(columns):
        return pl.BlockSpec((None, tokens, columns), lambda at: (at, 0, 0))

    def four(columns):
        return pl.BlockSpec((4, None, tokens, columns), lambda at: (0, at, 0, 0))

    def shape(columns, dtype):
        return jax.ShapeDtypeStruct((4, latents, tokens, columns), dtype)

    return pl.pallas_call(
        lambda *refs: attend_back_kernel(size, size**-0.5, *refs),
        grid=(latents,),
        in_specs=[block(triple)] * 8
        + [block(width)] * 4
        + [pl.BlockSpec((None, rows, heads), lambda at: (at, 0, 0))],
        out_specs=[four(width), four(2 * width), four(2 * width)],
        out_shape=[shape(width, LOW), shape(2 * width, FULL), shape(2 * width, FULL)],
        compiler_params=pltpu.CompilerParams(vmem_limit_bytes=VMEM_LIMIT),
        cost_estimate=pl.CostEstimate(
            flops=20 * latents * rows * rows * width,
            bytes_accessed=32 * latents * rows * width,
            transcendentals=2 * latents * heads * rows * rows,
        ),
        name="attention_backward",
    )(*own, *other, *grad, logsum)


class Weight:
    def __init__(self, unit, x_first):
        self.unit, self.x_first = unit, x_first

    def first(self, after=None):
        axis = "x" if self.x_first else "y"
        self.side = swap(tie(self.unit, after), **{axis: 1})

    def second(self, after=None):
        pair = jnp.concatenate([self.unit, self.side], axis=1)
        axis = "y" if self.x_first else "x"
        self.cross = swap(tie(pair, after), **{axis: 1})
        width = self.unit.shape[1]
        if self.x_first:
            parts = [self.unit, self.cross[:, :width], self.side, self.cross[:, width:]]
        else:
            parts = [pair, self.cross]
        self.near = jnp.concatenate(parts, axis=1)
        self.far = swap(self.near, core=1)

    def both(self):
        return (self.near, self.far)


class Grad:
    def __init__(self, near, far, width, x_first):
        self.near, self.width, self.x_first = near, width, x_first
        self.core = swap(far.astype(LOW), core=1)

    def term(self, unit):
        lo, hi = unit * self.width, (unit + 1) * self.width
        return self.near(lo, hi) + self.core[:, lo:hi].astype(FULL)

    def ready_first(self):
        if self.x_first:
            self.sent = jnp.concatenate(
                [self.term(1).astype(LOW), self.term(3).astype(LOW)], axis=1
            )
        else:
            lo, hi = 2 * self.width, 4 * self.width
            self.sent = (self.near(lo, hi) + self.core[:, lo:hi].astype(FULL)).astype(LOW)
        return self.sent

    def first(self, after=None):
        axis = "y" if self.x_first else "x"
        self.side = swap(tie(self.sent, after), **{axis: 1})

    def ready_second(self):
        sent = self.term(2 if self.x_first else 1) + self.side[:, self.width :].astype(FULL)
        self.sent = sent.astype(LOW)
        return self.sent

    def second(self, after=None):
        axis = "x" if self.x_first else "y"
        self.cross = swap(tie(self.sent, after), **{axis: 1})

    def unit(self):
        unit = self.term(0) + self.side[:, : self.width].astype(FULL)
        return unit + self.cross.astype(FULL)


def spread_ctx(place, unit):
    over_x = swap(unit, x=1)
    far = swap(jnp.stack([unit, over_x]), core=1)
    return unrelate([unit, far[0], over_x, far[1]], place.ctx)


def to_chips(place, blocks, after=None):
    arrived = []
    for at, (x, y) in enumerate(CHIPS):
        block = jnp.where(place.x ^ x == 0, blocks[y][0], blocks[y][1])
        arrived.append(block if at == 0 else swap(block, x=x, y=y))
    return arrived


def from_chips(place, blocks):
    arrived = [
        blocks[at] if at == 0 else swap(blocks[at], x=x, y=y) for at, (x, y) in enumerate(CHIPS)
    ]
    ordered = []
    for y in range(2):
        near, far = arrived[y], arrived[2 + y]
        ordered.append(jnp.where(place.x == 0, near, far))
        ordered.append(jnp.where(place.x == 0, far, near))
    return (ordered, arrived[1:])


def block_forward(place, resid, modulation, weights, biases, size, hook):
    (attn, up, down) = weights
    (query_bias, value_bias, proj_bias, up_bias, down_bias) = biases
    latents, tokens, width = resid.shape
    (shift_one, scale_one, gate_one, shift_two, scale_two, gate_two) = modulation
    normed_one, scaling_one = normalize(resid)
    entry_one = (normed_one * (1.0 + scale_one) + shift_one).astype(LOW).reshape(-1, width)
    (near, far) = attn.both()
    four = unrelate([near[:, :width], far[:, :width], near[:, width:], far[:, width:]], place.ctx)
    qkv_weight = jnp.concatenate(four[:3], axis=1)
    proj_weight = four[3]
    projected = dot(entry_one, qkv_weight)
    queries = (projected[:, :width] + query_bias).astype(LOW)
    keys = projected[:, width : 2 * width].astype(LOW)
    values = (projected[:, 2 * width :] + value_bias).astype(LOW)
    part = width // 4

    def block(at):
        members = [member[:, at * part : (at + 1) * part] for member in (keys, values, queries)]
        return jnp.concatenate(members, axis=1)

    own = to_chips(place, [[block(0), block(1)], [block(2), block(3)]])
    other = [swap(member, core=1) for member in own]
    hook("qkv", own[1:])
    own = [member.reshape(latents, tokens, -1) for member in own]
    other = [member.reshape(latents, tokens, -1) for member in other]
    attn_out, logsum = attend(own, other, size)
    pieces, arrived = from_chips(place, [member.reshape(-1, part) for member in attn_out])
    hook("out", arrived)
    context = jnp.concatenate(pieces, axis=1)
    attended = (dot_nt(context, proj_weight) + proj_bias).reshape(resid.shape)
    middle = resid + gate_one * attended
    normed_two, scaling_two = normalize(middle)
    entry_two = (normed_two * (1.0 + scale_two) + shift_two).astype(LOW).reshape(-1, width)
    up_pair, down_pair = up.both(), down.both()
    hidden_pre = [dot(entry_two, up_pair[at]) + up_bias[at] for at in range(2)]
    hidden = [activation(member).astype(LOW) for member in hidden_pre]
    mlp_out = dot_nt(hidden[0], down_pair[0]) + dot_nt(hidden[1], down_pair[1])
    mlp_out = (mlp_out + down_bias).reshape(resid.shape)
    result = middle + gate_two * mlp_out
    saved = (
        normed_one,
        scaling_one,
        entry_one,
        own,
        other,
        logsum,
        context,
        attended,
        normed_two,
        scaling_two,
        entry_two,
        hidden_pre,
        hidden,
        mlp_out,
        qkv_weight,
        proj_weight,
    )
    return (result, saved)


def block_backward(place, upstream, modulation, weights, saved, size, earlier):
    (attn, up, down) = weights
    (
        normed_one,
        scaling_one,
        entry_one,
        own,
        other,
        logsum,
        context,
        attended,
        normed_two,
        scaling_two,
        entry_two,
        hidden_pre,
        hidden,
        mlp_out,
        qkv_weight,
        proj_weight,
    ) = saved
    up_pair, down_pair = up.both(), down.both()
    latents, tokens, width = upstream.shape
    part = width // 4
    unit_width = width // 2
    (shift_one, scale_one, gate_one, shift_two, scale_two, gate_two) = modulation
    gate_two_grad = jnp.sum(upstream * mlp_out, axis=1)
    mlp_grad = (gate_two * upstream).astype(LOW).reshape(-1, width)
    down_bias_grad = jnp.sum(mlp_grad, axis=0, keepdims=True, dtype=FULL)
    down_grad = Grad(
        lambda lo, hi: dot_tn(mlp_grad, hidden[0][:, lo:hi]),
        dot_tn(mlp_grad, hidden[1]),
        unit_width,
        True,
    )
    pre_grad = []
    for at in (1, 0):
        unused_value, gelu_pull = jax.vjp(activation, hidden_pre[at])
        pre_grad.insert(0, gelu_pull(dot(mlp_grad, down_pair[at]))[0].astype(LOW))
    up_bias_grad = jnp.stack([jnp.sum(member, axis=0, dtype=FULL) for member in pre_grad])
    up_grad = Grad(
        lambda lo, hi: dot_tn(entry_two, pre_grad[0][:, lo:hi]),
        dot_tn(entry_two, pre_grad[1]),
        unit_width,
        False,
    )
    entry_two_grad = dot_nt(pre_grad[0], up_pair[0]) + dot_nt(pre_grad[1], up_pair[1])
    entry_two_grad = entry_two_grad.reshape(upstream.shape)
    scale_two_grad = jnp.sum(entry_two_grad * normed_two, axis=1)
    shift_two_grad = jnp.sum(entry_two_grad, axis=1)
    middle_grad = upstream + norm_back(entry_two_grad * (1.0 + scale_two), normed_two, scaling_two)
    gate_one_grad = jnp.sum(middle_grad * attended, axis=1)
    attended_grad = (gate_one * middle_grad).astype(LOW).reshape(-1, width)
    proj_bias_grad = jnp.sum(attended_grad, axis=0, keepdims=True, dtype=FULL)
    context_grad = dot(attended_grad, proj_weight).astype(LOW)
    blocks = [
        [context_grad[:, (2 * rel + at) * part : (2 * rel + at + 1) * part] for at in range(2)]
        for rel in range(2)
    ]
    if earlier is not None:
        blocks = tie(blocks, [earlier[0].side, earlier[1].cross, earlier[2].cross])
    out_grad = to_chips(place, blocks)
    ready = [down_grad.ready_first(), up_grad.ready_first()]
    down_grad.first(out_grad[1:])
    up_grad.first(out_grad[1:])
    if earlier is not None:
        ready.append(earlier[0].ready_second())
        earlier[0].second(out_grad[1:])
    out_grad = [member.reshape(latents, tokens, part) for member in out_grad]
    out_grad = tie(out_grad, ready)
    query_part, kv_own, kv_other = attend_back(own, other, out_grad, logsum, size)
    kv_part = (kv_own + swap(kv_other, core=1)).astype(LOW)
    blocks = [
        jnp.concatenate([kv_part[at], query_part[at]], axis=-1).reshape(-1, 3 * part)
        for at in range(4)
    ]
    due = [down_grad.side, up_grad.side]
    if earlier is not None:
        due.append(earlier[0].cross)
    pieces, arrived = from_chips(place, tie(blocks, due))
    ready = [down_grad.ready_second(), up_grad.ready_second()]
    down_grad.second(arrived)
    up_grad.second(arrived)
    pieces = tie(pieces, ready)
    triple = [
        jnp.concatenate([member[:, at * part : (at + 1) * part] for member in pieces], axis=1)
        for at in (2, 0, 1)
    ]
    query_bias_grad = jnp.sum(triple[0], axis=0, keepdims=True, dtype=FULL)
    value_bias_grad = jnp.sum(triple[2], axis=0, keepdims=True, dtype=FULL)
    entry_one_grad = dot_nt(jnp.concatenate(triple, axis=1), qkv_weight).reshape(upstream.shape)
    scale_one_grad = jnp.sum(entry_one_grad * normed_one, axis=1)
    shift_one_grad = jnp.sum(entry_one_grad, axis=1)
    resid_grad = middle_grad + norm_back(
        entry_one_grad * (1.0 + scale_one), normed_one, scaling_one
    )
    rights = jnp.stack([*triple, context])

    def attn_term(at, lo, hi):
        matrix = place.ctx ^ at
        left = jnp.where(matrix == 3, attended_grad, entry_one)
        right = lax.dynamic_index_in_dim(rights, matrix, 0, keepdims=False)
        return dot_tn(left, right[:, lo:hi])

    attn_grad = Grad(
        lambda lo, hi: attn_term(2, lo - width, hi - width) if lo >= width else attn_term(0, lo, hi),
        jnp.concatenate(
            [attn_term(1, 0, width).astype(LOW), attn_term(3, 0, width).astype(LOW)], axis=1
        ),
        unit_width,
        False,
    )
    attn_grad.ready_first()
    attn_grad.first()

    def halves(row):
        return jnp.concatenate(place.by_y(row[:, : width // 2], row[:, width // 2 :]), axis=1)

    up_rows = jnp.dot(
        place.unit_matrix(), up_bias_grad.reshape(8, unit_width), precision=PRECISE
    ).reshape(4, width)
    def placed(value, at):
        return jnp.pad(value, ((at, 8 - at - value.shape[0]), (0, 0)))

    biases = [halves(query_bias_grad), halves(value_bias_grad), proj_bias_grad, down_bias_grad]
    biases = sum(placed(member, at) for at, member in enumerate(biases)) + placed(up_rows, 4)
    spans = [
        shift_one_grad,
        scale_one_grad,
        gate_one_grad,
        shift_two_grad,
        scale_two_grad,
        gate_two_grad,
    ]
    small = jnp.concatenate([*[placed(member, 0) for member in spans], biases], axis=0)
    return (resid_grad, (attn_grad, up_grad, down_grad), small)


def local(
    mesh,
    latents_in,
    condition,
    out_grad,
    mod_weight,
    mod_bias,
    qkv_weight,
    qkv_bias,
    proj_weight,
    proj_bias,
    fc1_weight,
    fc1_bias,
    fc2_weight,
    fc2_bias,
):
    place = Place(mesh)
    n_dp = place.n_dp
    layers = mod_weight.shape[0]
    latents, ctx_tokens, width = latents_in.shape
    tokens = ctx_tokens // 2
    rows = width // n_dp
    heads = qkv_bias.shape[2]
    size = qkv_bias.shape[3] * n_dp
    quarter = fc1_weight.shape[2] // 4
    spans = mod_bias.shape[1]

    start = place.ctx * quarter
    quarters = []
    for layer in range(layers):
        attn = pick(place.ctx, [*[qkv_weight[layer, at] for at in range(3)], proj_weight[layer]])
        mlp = [
            lax.dynamic_slice_in_dim(member[layer], start, quarter, 1)
            for member in (fc1_weight, fc2_weight)
        ]
        quarters.append([attn, *mlp])
    attn = place.gather_dp(quarters[0][0]).reshape(width, quarter)
    after = lax.all_gather(jnp.stack(quarters[0][1:]), "dp", axis=1, tiled=True)
    packs = [[attn, after[0], after[1]]]
    for layer in range(1, layers):
        whole = tie(jnp.stack(quarters[layer]), after)
        after = lax.all_gather(whole, "dp", axis=1, tiled=True)
        packs.append([after[0], after[1], after[2]])
    weights = [
        (Weight(pack[0], False), Weight(pack[1], False), Weight(pack[2], True)) for pack in packs
    ]
    weights[0][0].first()
    weights[0][0].second()
    weights[0][1].first()
    weights[0][2].first(weights[0][0].cross)

    members = (mod_bias, qkv_bias, proj_bias, fc1_bias, fc2_bias)
    flat = jnp.concatenate(
        [condition.reshape(-1)] + [member.astype(FULL).reshape(-1) for member in members]
    )
    mine = place.gather_dp(flat)
    cond_all = mine[:, : condition.size].reshape(n_dp * latents, width)
    silu_all = jax.nn.silu(cond_all)
    silu_rows = lax.dynamic_slice_in_dim(silu_all, place.z * rows, rows, 1)
    mine = mine[:, condition.size :]
    pair = place.by_y(mine, swap(mine, y=1))
    everyone = jnp.stack(pair, axis=1)
    taken = []
    offset = 0
    for member in members:
        source = everyone if member.ndim > 2 and member is not mod_bias else mine
        part = lax.slice_in_dim(source, offset, offset + member.size, axis=-1)
        taken.append(part.reshape(source.shape[:-1] + member.shape))
        offset += member.size
    mod_bias_half = jnp.moveaxis(taken[0], 0, 2).reshape(layers, 1, spans * width)
    qkv_all = jnp.transpose(taken[1], (1, 2, 3, 4, 0, 5)).reshape(2, layers, 2, heads * size)
    qkv_bias_all = jnp.where(place.y == 0, qkv_all, qkv_all[::-1])
    proj_bias_all = jnp.moveaxis(taken[2], 0, 1).reshape(layers, width)
    fc1_all = jnp.transpose(taken[3], (2, 1, 3, 0, 4)).reshape(layers, 8, quarter)
    fc1_rel = jnp.einsum("ar,lae->lre", place.unit_matrix(), fc1_all, precision=PRECISE)
    fc2_bias_all = jnp.moveaxis(taken[4], 0, 1).reshape(layers, width)

    halfmod = jnp.einsum(
        "bd,lde->lbe", silu_rows, mod_weight.astype(FULL), precision=PRECISE
    ).reshape(layers, n_dp, latents, -1)
    halfmod = place.scatter_dp(
        lambda at: lax.dynamic_index_in_dim(halfmod, at, 1, keepdims=False), FULL
    )
    halfmod = halfmod + mod_bias_half
    by_half = place.by_y(halfmod, swap(halfmod, y=1))
    modulations = [
        [
            by_half[at // spans][layer, :, None, at % spans * width : (at % spans + 1) * width]
            for at in range(2 * spans)
        ]
        for layer in range(layers)
    ]

    token_start = place.y * tokens
    resid = lax.dynamic_slice_in_dim(latents_in, token_start, tokens, 1).astype(FULL)
    upstream = lax.dynamic_slice_in_dim(out_grad, token_start, tokens, 1).astype(FULL)
    saved_list = []
    all_biases = [
        (
            qkv_bias_all[:, layer, 0].reshape(1, -1),
            qkv_bias_all[:, layer, 1].reshape(1, -1),
            proj_bias_all[layer].reshape(1, -1),
            [fc1_rel[layer, 4 * core : 4 * core + 4].reshape(1, -1) for core in range(2)],
            fc2_bias_all[layer].reshape(1, -1),
        )
        for layer in range(layers)
    ]
    resid, modulations, all_biases = lax.optimization_barrier((resid, modulations, all_biases))
    for layer in range(layers):
        biases = all_biases[layer]

        def hook(event, arrived):
            if event == "qkv":
                for member in weights[layer][1:]:
                    member.second(arrived)
                if layer + 1 < layers:
                    weights[layer + 1][0].first(arrived)
                    weights[layer + 1][0].second()
            elif layer + 1 < layers:
                for member in weights[layer + 1][1:]:
                    member.first(arrived)

        resid, saved = block_forward(
            place, resid, modulations[layer], weights[layer], biases, size, hook
        )
        saved_list.append(saved)

    def both_halves(value):
        return jnp.concatenate(place.by_y(value, swap(value, y=1)), axis=1)

    block_out = both_halves(resid.astype(LOW))

    def scatter_units(members):
        units = jnp.concatenate([member.unit().astype(LOW) for member in members], axis=1)
        return lax.psum_scatter(units, "dp", scatter_dimension=0, tiled=True)

    shards = [None] * layers
    smalls = [None] * layers
    earlier = None
    for layer in reversed(range(layers)):
        upstream, grads, smalls[layer] = block_backward(
            place, upstream, modulations[layer], weights[layer], saved_list[layer], size, earlier
        )
        if earlier is not None:
            shards[layer + 1] = scatter_units(earlier)
        earlier = grads
    latents_grad = both_halves(upstream)
    (attn_grad, up_grad, down_grad) = earlier
    both = scatter_units([up_grad, down_grad])
    attn_grad.ready_second()
    attn_grad.second()
    attn = attn_grad.unit()
    attn = place.scatter_dp(
        lambda at: lax.dynamic_slice_in_dim(attn, at * rows, rows, 0), LOW
    ).astype(LOW)

    small = jnp.stack(smalls)
    small = small + swap(small, core=1)
    small = small + swap(small, y=1)
    small = place.gather_dp(small + swap(small, x=1))
    own_mod = lax.dynamic_slice_in_dim(small, place.y * 8 * spans, 8 * spans, 2)
    own_mod = own_mod.reshape(n_dp, layers, spans, 8, width)[:, :, :, :latents]
    own_mod = jnp.transpose(own_mod, (1, 0, 3, 2, 4)).reshape(layers, n_dp * latents, -1)
    mod_wgrad = jnp.einsum("bd,lbe->lde", silu_rows, own_mod, precision=PRECISE)
    mod_bsum = jnp.sum(own_mod, axis=1).reshape(layers, spans, width)
    mod_bgrad = lax.dynamic_slice_in_dim(mod_bsum, place.z * rows, rows, 2)
    cond_part = jnp.einsum("lbe,lde->bd", own_mod, mod_weight.astype(FULL), precision=PRECISE)
    bias_sum = jnp.sum(small[:, :, 16 * spans :], axis=0)
    cond_part = cond_part + swap(cond_part, y=1)
    cond_blocks = place.gather_dp(cond_part).reshape(n_dp, n_dp, latents, rows)
    cond_sum = lax.dynamic_index_in_dim(cond_blocks, place.z, 1, keepdims=False)
    cond_sum = jnp.moveaxis(cond_sum, 0, 1).reshape(latents, width)
    unused_value, silu_pull = jax.vjp(jax.nn.silu, condition)
    condition_grad = silu_pull(cond_sum)[0]

    qkv_b = bias_sum[:, :2].reshape(layers, 2, 2, heads, n_dp, -1)
    qkv_b = lax.dynamic_index_in_dim(qkv_b, place.y, 2, keepdims=False)
    qkv_bgrad = lax.dynamic_index_in_dim(qkv_b, place.z, 3, keepdims=False)
    out_b = lax.dynamic_slice_in_dim(bias_sum[:, 2:4], place.z * rows, rows, 2)
    fc1_b = bias_sum[:, 4:].reshape((layers, 2, fc1_bias.shape[1], n_dp, -1))
    fc1_b = lax.dynamic_index_in_dim(fc1_b, place.y, 1, keepdims=False)
    fc1_bgrad = lax.dynamic_index_in_dim(fc1_b, place.z, 2, keepdims=False)

    qkv_wgrad, proj_wgrad = [None] * layers, [None] * layers
    fc1_wgrad, fc2_wgrad = [None] * layers, [None] * layers
    for layer in range(layers):
        if layer > 0:
            units = spread_ctx(place, shards[layer])
            attn_units = [member[:, :quarter] for member in units]
            both_units = [member[:, quarter:] for member in units]
        else:
            both_units = spread_ctx(place, both)
            attn_units = spread_ctx(place, attn)
        qkv_wgrad[layer] = jnp.stack(attn_units[:3]).astype(FULL)
        proj_wgrad[layer] = attn_units[3].astype(FULL)
        fc1_wgrad[layer] = jnp.concatenate([member[:, :quarter] for member in both_units], axis=1)
        fc2_wgrad[layer] = jnp.concatenate([member[:, quarter:] for member in both_units], axis=1)
    return (
        block_out,
        latents_grad,
        condition_grad,
        mod_wgrad,
        mod_bgrad,
        jnp.stack(qkv_wgrad),
        qkv_bgrad,
        jnp.stack(proj_wgrad),
        out_b[:, 0],
        jnp.stack(fc1_wgrad).astype(FULL),
        fc1_bgrad,
        jnp.stack(fc2_wgrad).astype(FULL),
        out_b[:, 1],
    )


def solution(mesh):
    placed = (
        P("dp", "ctx", None),
        P("dp", None),
        P("dp", "ctx", None),
        P(None, "dp", "tp"),
        P(None, "tp", "dp"),
        P(None, None, "dp", "tp"),
        P(None, None, "tp", "dp"),
        P(None, "dp", "tp"),
        P(None, "dp"),
        P(None, "dp", "tp"),
        P(None, "tp", "dp"),
        P(None, "dp", "tp"),
        P(None, "dp"),
    )
    outs = (
        P("dp", "ctx", None),
        P("dp", "ctx", None),
        P("dp", None),
        P(None, "dp", "tp"),
        P(None, "tp", "dp"),
        P(None, None, "dp", "tp"),
        P(None, None, "tp", "dp"),
        P(None, "dp", "tp"),
        P(None, "dp"),
        P(None, "dp", "tp"),
        P(None, "tp", "dp"),
        P(None, "dp", "tp"),
        P(None, "dp"),
    )
    return jax.shard_map(
        lambda *arrays: local(mesh, *arrays),
        mesh=mesh,
        in_specs=placed,
        out_specs=outs,
        check_vma=False,
    )
```

```python
import jax
import jax.numpy as jnp
from jax import lax
from jax.experimental import pallas as pl
from jax.experimental.pallas import tpu as pltpu
from jax.sharding import PartitionSpec as P

PRECISE = lax.Precision.HIGHEST
EPSILON = 1e-06
LOW = jnp.bfloat16
FULL = jnp.float32
CHIPS = ((0, 0), (0, 1), (1, 0), (1, 1))
PLANE = ("ctx", "tp")
VMEM_LIMIT = 56 * 1024 * 1024


def swap(value, x=0, core=0, y=0):
    mask = 4 * x + 2 * core + y
    return lax.ppermute(value, PLANE, [(at, at ^ mask) for at in range(8)])


def swap_dp(value, mask, count):
    return lax.ppermute(value, "dp", [(at, at ^ mask) for at in range(count)])


def pick(index, options):
    if len(options) == 1:
        return options[0]
    half = len(options) // 2
    low, high = pick(index % half, options[:half]), pick(index % half, options[half:])
    return jnp.where(index // half == 0, low, high)


def tie(value, after):
    if after is None:
        return value
    return lax.optimization_barrier((value, after))[0]


def unrelate(pieces, index):
    return [pick(index, [pieces[place ^ at] for at in range(len(pieces))]) for place in range(len(pieces))]


class Place:
    def __init__(self, mesh):
        self.n_dp = mesh.shape["dp"]
        self.z = lax.axis_index("dp")
        self.ctx = lax.axis_index("ctx")
        self.x = self.ctx // 2
        self.core = self.ctx % 2
        self.y = lax.axis_index("tp")
        self.direct = self.n_dp <= 4 and self.n_dp & (self.n_dp - 1) == 0

    def gather_dp(self, value):
        if not self.direct:
            return lax.all_gather(value, "dp")
        pieces = [value] + [swap_dp(value, mask, self.n_dp) for mask in range(1, self.n_dp)]
        return jnp.stack(unrelate(pieces, self.z))

    def scatter_dp(self, parts, dtype):
        if not self.direct:
            whole = jnp.stack([parts(at) for at in range(self.n_dp)]).astype(dtype)
            return lax.psum_scatter(whole, "dp", scatter_dimension=0).astype(FULL)
        total = parts(self.z)
        for mask in range(1, self.n_dp):
            part = parts(self.z ^ mask).astype(dtype)
            total = total + swap_dp(part, mask, self.n_dp).astype(FULL)
        return total

    def by_y(self, near, far):
        return (jnp.where(self.y == 0, near, far), jnp.where(self.y == 0, far, near))

    def unit_matrix(self):
        at = lax.broadcasted_iota(jnp.int32, (8, 8), 0)
        rel = lax.broadcasted_iota(jnp.int32, (8, 8), 1)
        flip_core = (at % 2) ^ self.core
        flip_x = (at // 2 % 2) ^ self.x
        flip_y = (at // 4) ^ self.y
        return (rel == 4 * flip_core + 2 * flip_x + flip_y).astype(FULL)


def normalize(field):
    centre = field - jnp.mean(field, axis=-1, keepdims=True)
    scaling = lax.rsqrt(jnp.mean(centre * centre, axis=-1, keepdims=True) + EPSILON)
    return (centre * scaling, scaling)


def norm_back(upstream, normed, scaling):
    first = jnp.mean(upstream, axis=-1, keepdims=True)
    second = jnp.mean(upstream * normed, axis=-1, keepdims=True)
    return scaling * (upstream - first - normed * second)


def activation(field):
    return jax.nn.gelu(field, approximate=True)


def dot(left, right):
    return jnp.dot(left, right, preferred_element_type=FULL)


def dot_nt(left, right):
    return lax.dot_general(left, right, (((1,), (1,)), ((), ())), preferred_element_type=FULL)


def dot_tn(left, right):
    return lax.dot_general(left, right, (((0,), (0,)), ((), ())), preferred_element_type=FULL)


def attend_kernel(size, factor, *refs):
    own_refs, other_refs, out_refs, log_ref = refs[:4], refs[4:8], refs[8:12], refs[12]
    tokens, triple = own_refs[0].shape
    width = triple // 3
    own = jnp.concatenate([ref[...] for ref in own_refs], axis=0)
    other = jnp.concatenate([ref[:, : 2 * width] for ref in other_refs], axis=0)
    outs = []
    for head in range(width // size):
        lo, hi = head * size, (head + 1) * size
        queries = own[:, 2 * width + lo : 2 * width + hi] * jnp.asarray(factor, LOW)
        score_a = dot_nt(queries, own[:, lo:hi])
        score_b = dot_nt(queries, other[:, lo:hi])
        highest = jnp.maximum(
            jnp.max(score_a, axis=-1, keepdims=True), jnp.max(score_b, axis=-1, keepdims=True)
        )
        exp_a = jnp.exp(score_a - highest)
        exp_b = jnp.exp(score_b - highest)
        total = jnp.sum(exp_a, axis=-1, keepdims=True) + jnp.sum(exp_b, axis=-1, keepdims=True)
        inverse = 1.0 / total
        out = dot((exp_a * inverse).astype(LOW), own[:, width + lo : width + hi])
        out = out + dot((exp_b * inverse).astype(LOW), other[:, width + lo : width + hi])
        outs.append(out)
        log_ref[:, head : head + 1] = highest + jnp.log(total)
    out = jnp.concatenate(outs, axis=1).astype(LOW)
    for at in range(4):
        out_refs[at][...] = out[at * tokens : (at + 1) * tokens]


def attend(own, other, size):
    latents, tokens, triple = own[0].shape
    width = triple // 3
    heads = width // size
    rows = 4 * tokens

    def block(columns):
        return pl.BlockSpec((None, tokens, columns), lambda at: (at, 0, 0))

    results = pl.pallas_call(
        lambda *refs: attend_kernel(size, size**-0.5, *refs),
        grid=(latents,),
        in_specs=[block(triple)] * 8,
        out_specs=[block(width)] * 4 + [pl.BlockSpec((None, rows, heads), lambda at: (at, 0, 0))],
        out_shape=[jax.ShapeDtypeStruct((latents, tokens, width), LOW)] * 4
        + [jax.ShapeDtypeStruct((latents, rows, heads), FULL)],
        compiler_params=pltpu.CompilerParams(vmem_limit_bytes=VMEM_LIMIT),
        cost_estimate=pl.CostEstimate(
            flops=8 * latents * rows * rows * width,
            bytes_accessed=14 * latents * rows * width,
            transcendentals=2 * latents * heads * rows * rows,
        ),
        name="attention_forward",
    )(*own, *other)
    return (results[:4], results[4])


def attend_back_kernel(size, factor, *refs):
    own_refs, other_refs, grad_refs, log_ref = refs[:4], refs[4:8], refs[8:12], refs[12]
    query_ref, kv_own_ref, kv_other_ref = refs[13:]
    tokens, triple = own_refs[0].shape
    width = triple // 3
    rows = 4 * tokens
    own = jnp.concatenate([ref[...] for ref in own_refs], axis=0)
    other = jnp.concatenate([ref[:, : 2 * width] for ref in other_refs], axis=0)
    grad = jnp.concatenate([ref[...] for ref in grad_refs], axis=0)
    query_grads, key_own, value_own, key_other, value_other = [], [], [], [], []
    for head in range(width // size):
        lo, hi = head * size, (head + 1) * size
        queries = own[:, 2 * width + lo : 2 * width + hi] * jnp.asarray(factor, LOW)
        upstream = grad[:, lo:hi]
        logsum = log_ref[:, head : head + 1]
        keys_a = own[:, lo:hi]
        keys_b = other[:, lo:hi]
        prob_a = jnp.exp(dot_nt(queries, keys_a) - logsum)
        prob_b = jnp.exp(dot_nt(queries, keys_b) - logsum)
        grad_a = dot_nt(upstream, own[:, width + lo : width + hi])
        grad_b = dot_nt(upstream, other[:, width + lo : width + hi])
        terms = jnp.sum(prob_a * grad_a, axis=-1, keepdims=True)
        terms = terms + jnp.sum(prob_b * grad_b, axis=-1, keepdims=True)
        score_a = (prob_a * (grad_a - terms)).astype(LOW)
        score_b = (prob_b * (grad_b - terms)).astype(LOW)
        query_grads.append((dot(score_a, keys_a) + dot(score_b, keys_b)) * factor)
        key_own.append(dot_tn(score_a, queries))
        key_other.append(dot_tn(score_b, queries))
        value_own.append(dot_tn(prob_a.astype(LOW), upstream))
        value_other.append(dot_tn(prob_b.astype(LOW), upstream))
    query_ref[...] = jnp.concatenate(query_grads, axis=1).astype(LOW).reshape(4, tokens, width)
    kv_own_ref[...] = jnp.concatenate(key_own + value_own, axis=1).reshape(4, tokens, 2 * width)
    kv_other_ref[...] = jnp.concatenate(key_other + value_other, axis=1).reshape(
        4, tokens, 2 * width
    )


def attend_back(own, other, grad, logsum, size):
    latents, tokens, triple = own[0].shape
    width = triple // 3
    heads = width // size
    rows = 4 * tokens

    def block(columns):
        return pl.BlockSpec((None, tokens, columns), lambda at: (at, 0, 0))

    def four(columns):
        return pl.BlockSpec((4, None, tokens, columns), lambda at: (0, at, 0, 0))

    def shape(columns, dtype):
        return jax.ShapeDtypeStruct((4, latents, tokens, columns), dtype)

    return pl.pallas_call(
        lambda *refs: attend_back_kernel(size, size**-0.5, *refs),
        grid=(latents,),
        in_specs=[block(triple)] * 8
        + [block(width)] * 4
        + [pl.BlockSpec((None, rows, heads), lambda at: (at, 0, 0))],
        out_specs=[four(width), four(2 * width), four(2 * width)],
        out_shape=[shape(width, LOW), shape(2 * width, FULL), shape(2 * width, FULL)],
        compiler_params=pltpu.CompilerParams(vmem_limit_bytes=VMEM_LIMIT),
        cost_estimate=pl.CostEstimate(
            flops=20 * latents * rows * rows * width,
            bytes_accessed=32 * latents * rows * width,
            transcendentals=2 * latents * heads * rows * rows,
        ),
        name="attention_backward",
    )(*own, *other, *grad, logsum)


class Weight:
    def __init__(self, unit, x_first):
        self.unit, self.x_first = unit, x_first

    def first(self, after=None):
        axis = "x" if self.x_first else "y"
        self.side = swap(tie(self.unit, after), **{axis: 1})

    def second(self, after=None):
        pair = jnp.concatenate([self.unit, self.side], axis=1)
        axis = "y" if self.x_first else "x"
        self.cross = swap(tie(pair, after), **{axis: 1})
        width = self.unit.shape[1]
        if self.x_first:
            parts = [self.unit, self.cross[:, :width], self.side, self.cross[:, width:]]
        else:
            parts = [pair, self.cross]
        self.near = jnp.concatenate(parts, axis=1)
        self.far = swap(self.near, core=1)

    def both(self):
        return (self.near, self.far)


class Grad:
    def __init__(self, near, far, width, x_first):
        self.near, self.width, self.x_first = near, width, x_first
        self.core = swap(far.astype(LOW), core=1)

    def term(self, unit):
        lo, hi = unit * self.width, (unit + 1) * self.width
        return self.near(lo, hi) + self.core[:, lo:hi].astype(FULL)

    def ready_first(self):
        if self.x_first:
            self.sent = jnp.concatenate(
                [self.term(1).astype(LOW), self.term(3).astype(LOW)], axis=1
            )
        else:
            lo, hi = 2 * self.width, 4 * self.width
            self.sent = (self.near(lo, hi) + self.core[:, lo:hi].astype(FULL)).astype(LOW)
        return self.sent

    def first(self, after=None):
        axis = "y" if self.x_first else "x"
        self.side = swap(tie(self.sent, after), **{axis: 1})

    def ready_second(self):
        sent = self.term(2 if self.x_first else 1) + self.side[:, self.width :].astype(FULL)
        self.sent = sent.astype(LOW)
        return self.sent

    def second(self, after=None):
        axis = "x" if self.x_first else "y"
        self.cross = swap(tie(self.sent, after), **{axis: 1})

    def unit(self):
        unit = self.term(0) + self.side[:, : self.width].astype(FULL)
        return unit + self.cross.astype(FULL)


def spread_ctx(place, unit):
    over_x = swap(unit, x=1)
    far = swap(jnp.stack([unit, over_x]), core=1)
    return unrelate([unit, far[0], over_x, far[1]], place.ctx)


def to_chips(place, blocks, after=None):
    arrived = []
    for at, (x, y) in enumerate(CHIPS):
        block = jnp.where(place.x ^ x == 0, blocks[y][0], blocks[y][1])
        arrived.append(block if at == 0 else swap(block, x=x, y=y))
    return arrived


def from_chips(place, blocks):
    arrived = [
        blocks[at] if at == 0 else swap(blocks[at], x=x, y=y) for at, (x, y) in enumerate(CHIPS)
    ]
    ordered = []
    for y in range(2):
        near, far = arrived[y], arrived[2 + y]
        ordered.append(jnp.where(place.x == 0, near, far))
        ordered.append(jnp.where(place.x == 0, far, near))
    return (ordered, arrived[1:])


def block_forward(place, resid, modulation, weights, biases, size, hook):
    (attn, up, down) = weights
    (query_bias, value_bias, proj_bias, up_bias, down_bias) = biases
    latents, tokens, width = resid.shape
    (shift_one, scale_one, gate_one, shift_two, scale_two, gate_two) = modulation
    normed_one, scaling_one = normalize(resid)
    entry_one = (normed_one * (1.0 + scale_one) + shift_one).astype(LOW).reshape(-1, width)
    (near, far) = attn.both()
    four = unrelate([near[:, :width], far[:, :width], near[:, width:], far[:, width:]], place.ctx)
    qkv_weight = jnp.concatenate(four[:3], axis=1)
    proj_weight = four[3]
    projected = dot(entry_one, qkv_weight)
    queries = (projected[:, :width] + query_bias).astype(LOW)
    keys = projected[:, width : 2 * width].astype(LOW)
    values = (projected[:, 2 * width :] + value_bias).astype(LOW)
    part = width // 4

    def block(at):
        members = [member[:, at * part : (at + 1) * part] for member in (keys, values, queries)]
        return jnp.concatenate(members, axis=1)

    own = to_chips(place, [[block(0), block(1)], [block(2), block(3)]])
    other = [swap(member, core=1) for member in own]
    hook("qkv", own[1:])
    own = [member.reshape(latents, tokens, -1) for member in own]
    other = [member.reshape(latents, tokens, -1) for member in other]
    attn_out, logsum = attend(own, other, size)
    pieces, arrived = from_chips(place, [member.reshape(-1, part) for member in attn_out])
    hook("out", arrived)
    context = jnp.concatenate(pieces, axis=1)
    attended = (dot_nt(context, proj_weight) + proj_bias).reshape(resid.shape)
    middle = resid + gate_one * attended
    normed_two, scaling_two = normalize(middle)
    entry_two = (normed_two * (1.0 + scale_two) + shift_two).astype(LOW).reshape(-1, width)
    up_pair, down_pair = up.both(), down.both()
    hidden_pre = [dot(entry_two, up_pair[at]) + up_bias[at] for at in range(2)]
    hidden = [activation(member).astype(LOW) for member in hidden_pre]
    mlp_out = dot_nt(hidden[0], down_pair[0]) + dot_nt(hidden[1], down_pair[1])
    mlp_out = (mlp_out + down_bias).reshape(resid.shape)
    result = middle + gate_two * mlp_out
    saved = (
        normed_one,
        scaling_one,
        entry_one,
        own,
        other,
        logsum,
        context,
        attended,
        normed_two,
        scaling_two,
        entry_two,
        hidden_pre,
        hidden,
        mlp_out,
        qkv_weight,
        proj_weight,
    )
    return (result, saved)


def block_backward(place, upstream, modulation, weights, saved, size, earlier):
    (attn, up, down) = weights
    (
        normed_one,
        scaling_one,
        entry_one,
        own,
        other,
        logsum,
        context,
        attended,
        normed_two,
        scaling_two,
        entry_two,
        hidden_pre,
        hidden,
        mlp_out,
        qkv_weight,
        proj_weight,
    ) = saved
    up_pair, down_pair = up.both(), down.both()
    latents, tokens, width = upstream.shape
    part = width // 4
    unit_width = width // 2
    (shift_one, scale_one, gate_one, shift_two, scale_two, gate_two) = modulation
    gate_two_grad = jnp.sum(upstream * mlp_out, axis=1)
    mlp_grad = (gate_two * upstream).astype(LOW).reshape(-1, width)
    down_bias_grad = jnp.sum(mlp_grad, axis=0, keepdims=True, dtype=FULL)
    down_grad = Grad(
        lambda lo, hi: dot_tn(mlp_grad, hidden[0][:, lo:hi]),
        dot_tn(mlp_grad, hidden[1]),
        unit_width,
        True,
    )
    pre_grad = []
    for at in (1, 0):
        unused_value, gelu_pull = jax.vjp(activation, hidden_pre[at])
        pre_grad.insert(0, gelu_pull(dot(mlp_grad, down_pair[at]))[0].astype(LOW))
    up_bias_grad = jnp.stack([jnp.sum(member, axis=0, dtype=FULL) for member in pre_grad])
    up_grad = Grad(
        lambda lo, hi: dot_tn(entry_two, pre_grad[0][:, lo:hi]),
        dot_tn(entry_two, pre_grad[1]),
        unit_width,
        False,
    )
    entry_two_grad = dot_nt(pre_grad[0], up_pair[0]) + dot_nt(pre_grad[1], up_pair[1])
    entry_two_grad = entry_two_grad.reshape(upstream.shape)
    scale_two_grad = jnp.sum(entry_two_grad * normed_two, axis=1)
    shift_two_grad = jnp.sum(entry_two_grad, axis=1)
    middle_grad = upstream + norm_back(entry_two_grad * (1.0 + scale_two), normed_two, scaling_two)
    gate_one_grad = jnp.sum(middle_grad * attended, axis=1)
    attended_grad = (gate_one * middle_grad).astype(LOW).reshape(-1, width)
    proj_bias_grad = jnp.sum(attended_grad, axis=0, keepdims=True, dtype=FULL)
    context_grad = dot(attended_grad, proj_weight).astype(LOW)
    blocks = [
        [context_grad[:, (2 * rel + at) * part : (2 * rel + at + 1) * part] for at in range(2)]
        for rel in range(2)
    ]
    if earlier is not None:
        blocks = tie(blocks, [earlier[1].cross, earlier[2].cross])
    out_grad = to_chips(place, blocks)
    ready = [down_grad.ready_first(), up_grad.ready_first()]
    down_grad.first(out_grad[1:])
    up_grad.first(out_grad[1:])
    if earlier is not None:
        ready.append(earlier[0].ready_second())
        ready.append(earlier[0].side)
        earlier[0].second(out_grad[1:])
    out_grad = [member.reshape(latents, tokens, part) for member in out_grad]
    out_grad = tie(out_grad, ready)
    query_part, kv_own, kv_other = attend_back(own, other, out_grad, logsum, size)
    kv_part = (kv_own + swap(kv_other, core=1)).astype(LOW)
    blocks = [
        jnp.concatenate([kv_part[at], query_part[at]], axis=-1).reshape(-1, 3 * part)
        for at in range(4)
    ]
    due = [down_grad.side, up_grad.side]
    if earlier is not None:
        due.append(earlier[0].cross)
    pieces, arrived = from_chips(place, tie(blocks, due))
    ready = [down_grad.ready_second(), up_grad.ready_second()]
    down_grad.second(arrived)
    up_grad.second(arrived)
    pieces = tie(pieces, ready)
    triple = [
        jnp.concatenate([member[:, at * part : (at + 1) * part] for member in pieces], axis=1)
        for at in (2, 0, 1)
    ]
    query_bias_grad = jnp.sum(triple[0], axis=0, keepdims=True, dtype=FULL)
    value_bias_grad = jnp.sum(triple[2], axis=0, keepdims=True, dtype=FULL)
    entry_one_grad = dot_nt(jnp.concatenate(triple, axis=1), qkv_weight).reshape(upstream.shape)
    scale_one_grad = jnp.sum(entry_one_grad * normed_one, axis=1)
    shift_one_grad = jnp.sum(entry_one_grad, axis=1)
    resid_grad = middle_grad + norm_back(
        entry_one_grad * (1.0 + scale_one), normed_one, scaling_one
    )
    rights = jnp.stack([*triple, context])

    def attn_term(at, lo, hi):
        matrix = place.ctx ^ at
        left = jnp.where(matrix == 3, attended_grad, entry_one)
        right = lax.dynamic_index_in_dim(rights, matrix, 0, keepdims=False)
        return dot_tn(left, right[:, lo:hi])

    attn_grad = Grad(
        lambda lo, hi: attn_term(2, lo - width, hi - width) if lo >= width else attn_term(0, lo, hi),
        jnp.concatenate(
            [attn_term(1, 0, width).astype(LOW), attn_term(3, 0, width).astype(LOW)], axis=1
        ),
        unit_width,
        False,
    )
    attn_grad.ready_first()
    attn_grad.first()

    def halves(row):
        return jnp.concatenate(place.by_y(row[:, : width // 2], row[:, width // 2 :]), axis=1)

    up_rows = jnp.dot(
        place.unit_matrix(), up_bias_grad.reshape(8, unit_width), precision=PRECISE
    ).reshape(4, width)
    def placed(value, at):
        return jnp.pad(value, ((at, 8 - at - value.shape[0]), (0, 0)))

    biases = [halves(query_bias_grad), halves(value_bias_grad), proj_bias_grad, down_bias_grad]
    biases = sum(placed(member, at) for at, member in enumerate(biases)) + placed(up_rows, 4)
    spans = [
        shift_one_grad,
        scale_one_grad,
        gate_one_grad,
        shift_two_grad,
        scale_two_grad,
        gate_two_grad,
    ]
    small = jnp.concatenate([*[placed(member, 0) for member in spans], biases], axis=0)
    return (resid_grad, (attn_grad, up_grad, down_grad), small)


def local(
    mesh,
    latents_in,
    condition,
    out_grad,
    mod_weight,
    mod_bias,
    qkv_weight,
    qkv_bias,
    proj_weight,
    proj_bias,
    fc1_weight,
    fc1_bias,
    fc2_weight,
    fc2_bias,
):
    place = Place(mesh)
    n_dp = place.n_dp
    layers = mod_weight.shape[0]
    latents, ctx_tokens, width = latents_in.shape
    tokens = ctx_tokens // 2
    rows = width // n_dp
    heads = qkv_bias.shape[2]
    size = qkv_bias.shape[3] * n_dp
    quarter = fc1_weight.shape[2] // 4
    spans = mod_bias.shape[1]

    start = place.ctx * quarter
    quarters = []
    for layer in range(layers):
        attn = pick(place.ctx, [*[qkv_weight[layer, at] for at in range(3)], proj_weight[layer]])
        mlp = [
            lax.dynamic_slice_in_dim(member[layer], start, quarter, 1)
            for member in (fc1_weight, fc2_weight)
        ]
        quarters.append([attn, *mlp])
    attn = place.gather_dp(quarters[0][0]).reshape(width, quarter)
    after = lax.all_gather(jnp.stack(quarters[0][1:]), "dp", axis=1, tiled=True)
    packs = [[attn, after[0], after[1]]]
    for layer in range(1, layers):
        whole = tie(jnp.stack(quarters[layer]), after)
        after = lax.all_gather(whole, "dp", axis=1, tiled=True)
        packs.append([after[0], after[1], after[2]])
    weights = [
        (Weight(pack[0], False), Weight(pack[1], False), Weight(pack[2], True)) for pack in packs
    ]
    weights[0][0].first()
    weights[0][0].second()
    weights[0][1].first()
    weights[0][2].first(weights[0][0].cross)

    members = (mod_bias, qkv_bias, proj_bias, fc1_bias, fc2_bias)
    flat = jnp.concatenate(
        [condition.reshape(-1)] + [member.astype(FULL).reshape(-1) for member in members]
    )
    mine = place.gather_dp(flat)
    cond_all = mine[:, : condition.size].reshape(n_dp * latents, width)
    silu_all = jax.nn.silu(cond_all)
    silu_rows = lax.dynamic_slice_in_dim(silu_all, place.z * rows, rows, 1)
    mine = mine[:, condition.size :]
    pair = place.by_y(mine, swap(mine, y=1))
    everyone = jnp.stack(pair, axis=1)
    taken = []
    offset = 0
    for member in members:
        source = everyone if member.ndim > 2 and member is not mod_bias else mine
        part = lax.slice_in_dim(source, offset, offset + member.size, axis=-1)
        taken.append(part.reshape(source.shape[:-1] + member.shape))
        offset += member.size
    mod_bias_half = jnp.moveaxis(taken[0], 0, 2).reshape(layers, 1, spans * width)
    qkv_all = jnp.transpose(taken[1], (1, 2, 3, 4, 0, 5)).reshape(2, layers, 2, heads * size)
    qkv_bias_all = jnp.where(place.y == 0, qkv_all, qkv_all[::-1])
    proj_bias_all = jnp.moveaxis(taken[2], 0, 1).reshape(layers, width)
    fc1_all = jnp.transpose(taken[3], (2, 1, 3, 0, 4)).reshape(layers, 8, quarter)
    fc1_rel = jnp.einsum("ar,lae->lre", place.unit_matrix(), fc1_all, precision=PRECISE)
    fc2_bias_all = jnp.moveaxis(taken[4], 0, 1).reshape(layers, width)

    halfmod = jnp.einsum(
        "bd,lde->lbe", silu_rows, mod_weight.astype(FULL), precision=PRECISE
    ).reshape(layers, n_dp, latents, -1)
    halfmod = place.scatter_dp(
        lambda at: lax.dynamic_index_in_dim(halfmod, at, 1, keepdims=False), FULL
    )
    halfmod = halfmod + mod_bias_half
    by_half = place.by_y(halfmod, swap(halfmod, y=1))
    modulations = [
        [
            by_half[at // spans][layer, :, None, at % spans * width : (at % spans + 1) * width]
            for at in range(2 * spans)
        ]
        for layer in range(layers)
    ]

    token_start = place.y * tokens
    resid = lax.dynamic_slice_in_dim(latents_in, token_start, tokens, 1).astype(FULL)
    upstream = lax.dynamic_slice_in_dim(out_grad, token_start, tokens, 1).astype(FULL)
    saved_list = []
    all_biases = [
        (
            qkv_bias_all[:, layer, 0].reshape(1, -1),
            qkv_bias_all[:, layer, 1].reshape(1, -1),
            proj_bias_all[layer].reshape(1, -1),
            [fc1_rel[layer, 4 * core : 4 * core + 4].reshape(1, -1) for core in range(2)],
            fc2_bias_all[layer].reshape(1, -1),
        )
        for layer in range(layers)
    ]
    resid, modulations, all_biases = lax.optimization_barrier((resid, modulations, all_biases))
    for layer in range(layers):
        biases = all_biases[layer]

        def hook(event, arrived):
            if event == "qkv":
                for member in weights[layer][1:]:
                    member.second(arrived)
                if layer + 1 < layers:
                    weights[layer + 1][0].first(arrived)
                    weights[layer + 1][0].second()
            elif layer + 1 < layers:
                for member in weights[layer + 1][1:]:
                    member.first(arrived)

        resid, saved = block_forward(
            place, resid, modulations[layer], weights[layer], biases, size, hook
        )
        saved_list.append(saved)

    def both_halves(value):
        return jnp.concatenate(place.by_y(value, swap(value, y=1)), axis=1)

    block_out = both_halves(resid.astype(LOW))

    def scatter_units(members):
        units = jnp.concatenate([member.unit().astype(LOW) for member in members], axis=1)
        return lax.psum_scatter(units, "dp", scatter_dimension=0, tiled=True)

    shards = [None] * layers
    smalls = [None] * layers
    earlier = None
    for layer in reversed(range(layers)):
        upstream, grads, smalls[layer] = block_backward(
            place, upstream, modulations[layer], weights[layer], saved_list[layer], size, earlier
        )
        if earlier is not None:
            shards[layer + 1] = scatter_units(earlier)
        earlier = grads
    latents_grad = both_halves(upstream)
    (attn_grad, up_grad, down_grad) = earlier
    both = scatter_units([up_grad, down_grad])
    first_sent = attn_grad.sent
    attn_grad.ready_second()
    attn_grad.second()
    attn = attn_grad.unit()
    attn = place.scatter_dp(
        lambda at: lax.dynamic_slice_in_dim(attn, at * rows, rows, 0), LOW
    ).astype(LOW)

    small = tie(jnp.stack(smalls), first_sent)
    small = small + swap(small, core=1)
    small = small + swap(small, y=1)
    small = place.gather_dp(tie(small + swap(small, x=1), attn_grad.cross))
    own_mod = lax.dynamic_slice_in_dim(small, place.y * 8 * spans, 8 * spans, 2)
    own_mod = own_mod.reshape(n_dp, layers, spans, 8, width)[:, :, :, :latents]
    own_mod = jnp.transpose(own_mod, (1, 0, 3, 2, 4)).reshape(layers, n_dp * latents, -1)
    mod_wgrad = jnp.einsum("bd,lbe->lde", silu_rows, own_mod, precision=PRECISE)
    mod_bsum = jnp.sum(own_mod, axis=1).reshape(layers, spans, width)
    mod_bgrad = lax.dynamic_slice_in_dim(mod_bsum, place.z * rows, rows, 2)
    cond_part = jnp.einsum("lbe,lde->bd", own_mod, mod_weight.astype(FULL), precision=PRECISE)
    bias_sum = jnp.sum(small[:, :, 16 * spans :], axis=0)
    cond_part = cond_part + swap(cond_part, y=1)
    cond_blocks = place.gather_dp(cond_part).reshape(n_dp, n_dp, latents, rows)
    cond_sum = lax.dynamic_index_in_dim(cond_blocks, place.z, 1, keepdims=False)
    cond_sum = jnp.moveaxis(cond_sum, 0, 1).reshape(latents, width)
    unused_value, silu_pull = jax.vjp(jax.nn.silu, condition)
    condition_grad = silu_pull(cond_sum)[0]

    qkv_b = bias_sum[:, :2].reshape(layers, 2, 2, heads, n_dp, -1)
    qkv_b = lax.dynamic_index_in_dim(qkv_b, place.y, 2, keepdims=False)
    qkv_bgrad = lax.dynamic_index_in_dim(qkv_b, place.z, 3, keepdims=False)
    out_b = lax.dynamic_slice_in_dim(bias_sum[:, 2:4], place.z * rows, rows, 2)
    fc1_b = bias_sum[:, 4:].reshape((layers, 2, fc1_bias.shape[1], n_dp, -1))
    fc1_b = lax.dynamic_index_in_dim(fc1_b, place.y, 1, keepdims=False)
    fc1_bgrad = lax.dynamic_index_in_dim(fc1_b, place.z, 2, keepdims=False)

    qkv_wgrad, proj_wgrad = [None] * layers, [None] * layers
    fc1_wgrad, fc2_wgrad = [None] * layers, [None] * layers
    for layer in range(layers):
        if layer > 0:
            units = spread_ctx(place, shards[layer])
            attn_units = [member[:, :quarter] for member in units]
            both_units = [member[:, quarter:] for member in units]
        else:
            both_units = spread_ctx(place, both)
            attn_units = spread_ctx(place, attn)
        qkv_wgrad[layer] = jnp.stack(attn_units[:3]).astype(FULL)
        proj_wgrad[layer] = attn_units[3].astype(FULL)
        fc1_wgrad[layer] = jnp.concatenate([member[:, :quarter] for member in both_units], axis=1)
        fc2_wgrad[layer] = jnp.concatenate([member[:, quarter:] for member in both_units], axis=1)
    return (
        block_out,
        latents_grad,
        condition_grad,
        mod_wgrad,
        mod_bgrad,
        jnp.stack(qkv_wgrad),
        qkv_bgrad,
        jnp.stack(proj_wgrad),
        out_b[:, 0],
        jnp.stack(fc1_wgrad).astype(FULL),
        fc1_bgrad,
        jnp.stack(fc2_wgrad).astype(FULL),
        out_b[:, 1],
    )


def solution(mesh):
    placed = (
        P("dp", "ctx", None),
        P("dp", None),
        P("dp", "ctx", None),
        P(None, "dp", "tp"),
        P(None, "tp", "dp"),
        P(None, None, "dp", "tp"),
        P(None, None, "tp", "dp"),
        P(None, "dp", "tp"),
        P(None, "dp"),
        P(None, "dp", "tp"),
        P(None, "tp", "dp"),
        P(None, "dp", "tp"),
        P(None, "dp"),
    )
    outs = (
        P("dp", "ctx", None),
        P("dp", "ctx", None),
        P("dp", None),
        P(None, "dp", "tp"),
        P(None, "tp", "dp"),
        P(None, None, "dp", "tp"),
        P(None, None, "tp", "dp"),
        P(None, "dp", "tp"),
        P(None, "dp"),
        P(None, "dp", "tp"),
        P(None, "tp", "dp"),
        P(None, "dp", "tp"),
        P(None, "dp"),
    )
    return jax.shard_map(
        lambda *arrays: local(mesh, *arrays),
        mesh=mesh,
        in_specs=placed,
        out_specs=outs,
        check_vma=False,
    )
```
